128 devices in a mesh: dp: 8 (over x, core), param: 16 (over z, y).
Axes of the slice: x: 4, y: 4, z: 4, core: 2. Of those that a mesh axis runs over, the one named last changes fastest.
Arguments:
- activations: bfloat16 [48, 2048, 8192], P('dp', None, 'param'), may hold values from -6 to 6
- output_gradient_rows: bfloat16 [48, 2048, 8192], P('dp', None, 'param'), may hold values from -0.19921875 to 0.19921875
- lengths: int32 [48], P('dp'), may hold values from 512 to 2048, as said below
- shrinking_factor: bfloat16 [8192, 128], P('param', 'dp'), may hold values from -0.0625 to 0.0625
- expanding_factor: bfloat16 [128, 8192], P('dp', 'param'), may hold values from -0.0625 to 0.0625
- shrinking_running_average: float32 [8192, 128], P('param', 'dp'), may hold values from -0.6 to 0.6
- shrinking_running_variance: float32 [8192, 128], P('param', 'dp'), may hold values from 0.01 to 1
- expanding_running_average: float32 [128, 8192], P('dp', 'param'), may hold values from -0.6 to 0.6
- expanding_running_variance: float32 [128, 8192], P('dp', 'param'), may hold values from 0.01 to 1
- up_rank_projector: float32 [128, 64], replicated
- up_width_projector: float32 [8192, 64], P('param'), may hold values from -0.0625 to 0.0625
- down_width_projector: float32 [8192, 64], P('param'), may hold values from -0.0625 to 0.0625
- down_rank_projector: float32 [128, 64], replicated
Outputs:
- features: float32 [48, 8192], P('dp', 'param')
The draws below stay inside these ranges and needn't reach their ends.
Inputs may be any that keep to these rules, and one draw needn't show every extreme that they name: `lengths`: some example has 2048 valid tokens and some has 512.
All inputs are finite; a program needn't handle non-finite values.
Results may differ from the reference program's by a relative error of at most 0.00045.
Values may be sent and summed in bfloat16 or wider, within the bound.
No kernel may reach another device: no remote copies, remote signals or barrier semaphores. Data moves between devices by JAX's collectives and lax.ppermute only.
A program may use at most 128 MiB of HBM per device.

```python
import math
import jax
import jax.numpy as jnp
from jax import lax

HIDDEN_SIZE = 8192
FACTOR_INNER_DIM = 128
SKETCH_EXTENT = 64
TOK = 2048
EXAMPLES = 48


def column_scaled(key, spread):
    starting_offset = jax.random.normal(key, (FACTOR_INNER_DIM, SKETCH_EXTENT), jnp.float32) / jnp.sqrt(jnp.float32(FACTOR_INNER_DIM))
    ramp = 3.0 ** (jnp.arange(SKETCH_EXTENT, dtype=jnp.float32) / (SKETCH_EXTENT - 1))
    extra = jnp.exp(jax.random.uniform(jax.random.fold_in(key, 9), (SKETCH_EXTENT,), jnp.float32) * jnp.log(jnp.float32(spread)))
    return starting_offset * (ramp * extra)[None, :]


def draw_up_rank_projector(key, part):
    key = jax.random.fold_in(key, 1)
    return column_scaled(key, 1.0)


def draw_down_rank_projector(key, part):
    key = jax.random.fold_in(key, 2)
    return column_scaled(key, 1.0)


def draw_lengths(key, part):
    key = jax.random.fold_in(key, 3)
    counts = jax.random.randint(key, (EXAMPLES,), TOK // 4, TOK + 1)
    counts = counts.at[0].set(TOK)
    return counts.at[1].set(TOK // 4).astype(jnp.int32)


def level_of(key, extent, cuts, least, high):
    gain = 1.0
    for position, parts in cuts:
        heights = jax.random.uniform(jax.random.fold_in(jax.random.fold_in(key, 6), position), (parts,), jnp.float32, least / len(cuts), high / len(cuts))
        gain = gain * jnp.repeat(jnp.exp(heights), extent[position] // parts).reshape((-1,) + (1,) * (len(extent) - 1 - position))
    return gain


def scatter_about(key, extent, deviation, most, pieces=(), kind=jnp.bfloat16):
    factor_of = level_of(key, extent, pieces, -0.22, 0.18) if pieces else 1.0
    array = jax.random.normal(key, extent, jnp.float32) * deviation * factor_of
    return jnp.minimum(jnp.maximum(array, -most), most).astype(kind)


def setup_inputs(seed: int = 0) -> dict:
    seeds = jax.random.split(jax.random.key(seed), 14)
    activations = scatter_about(seeds[0], (EXAMPLES, TOK, HIDDEN_SIZE), 1.0, 6.0, ((0, 8), (2, 16)))
    output_gradient_rows = scatter_about(seeds[1], (EXAMPLES, TOK, HIDDEN_SIZE), 0.03, 0.19921875, ((0, 8), (2, 16)))
    lengths = draw_lengths(jax.random.fold_in(seeds[13], 71), 0)
    shrinking_factor = scatter_about(seeds[3], (HIDDEN_SIZE, FACTOR_INNER_DIM), HIDDEN_SIZE ** -0.5, 0.0625, ((0, 16), (1, 8)))
    expanding_factor = scatter_about(seeds[4], (FACTOR_INNER_DIM, HIDDEN_SIZE), HIDDEN_SIZE ** -0.5, 0.0625, ((0, 8), (1, 16)))
    shrinking_running_average = scatter_about(seeds[5], (HIDDEN_SIZE, FACTOR_INNER_DIM), 0.1, 0.6, ((0, 16), (1, 8)), jnp.float32)
    shrinking_running_variance = jnp.clip(jnp.exp(math.log(1.0) - 4.6051702 * jax.random.uniform(seeds[6], (HIDDEN_SIZE, FACTOR_INNER_DIM), jnp.float32) ** level_of(seeds[6], (HIDDEN_SIZE, FACTOR_INNER_DIM), ((0, 16), (1, 8)), -0.2, 0.2)), 0.01, 1.0)
    expanding_running_average = scatter_about(seeds[7], (FACTOR_INNER_DIM, HIDDEN_SIZE), 0.1, 0.6, ((0, 8), (1, 16)), jnp.float32)
    expanding_running_variance = jnp.clip(jnp.exp(math.log(1.0) - 4.6051702 * jax.random.uniform(seeds[8], (FACTOR_INNER_DIM, HIDDEN_SIZE), jnp.float32) ** level_of(seeds[8], (FACTOR_INNER_DIM, HIDDEN_SIZE), ((0, 8), (1, 16)), -0.2, 0.2)), 0.01, 1.0)
    up_rank_projector = draw_up_rank_projector(jax.random.fold_in(seeds[13], 71), 0)
    up_width_projector = scatter_about(seeds[10], (HIDDEN_SIZE, SKETCH_EXTENT), HIDDEN_SIZE ** -0.5, 0.0625, ((0, 16),), jnp.float32)
    down_width_projector = scatter_about(seeds[11], (HIDDEN_SIZE, SKETCH_EXTENT), HIDDEN_SIZE ** -0.5, 0.0625, ((0, 16),), jnp.float32)
    down_rank_projector = draw_down_rank_projector(jax.random.fold_in(seeds[13], 71), 0)
    return dict(activations=activations, output_gradient_rows=output_gradient_rows, lengths=lengths, shrinking_factor=shrinking_factor, expanding_factor=expanding_factor, shrinking_running_average=shrinking_running_average, shrinking_running_variance=shrinking_running_variance, expanding_running_average=expanding_running_average, expanding_running_variance=expanding_running_variance, up_rank_projector=up_rank_projector, up_width_projector=up_width_projector, down_width_projector=down_width_projector, down_rank_projector=down_rank_projector)


def precondition(grad, first, second):
    top = 0.9 * first + 0.1 * grad
    return top / (jnp.sqrt(0.999 * second + 0.001 * grad * grad) + 1e-08)

def reference(activations, output_gradient_rows, lengths, shrinking_factor, expanding_factor, shrinking_running_average, shrinking_running_variance, expanding_running_average, expanding_running_variance, up_rank_projector, up_width_projector, down_width_projector, down_rank_projector):
    positions = jnp.arange(TOK, dtype=jnp.int32)
    high = lax.Precision.HIGHEST

    def one_example(items):
        input_rows, gradient_list, count = items
        valid_mask = (positions < count)[:, None]
        lowered_program = jnp.where(valid_mask, jnp.dot(input_rows, shrinking_factor, preferred_element_type=jnp.float32), 0.0).astype(jnp.bfloat16)
        raised_error = jnp.where(valid_mask, jnp.dot(gradient_list, expanding_factor.T, preferred_element_type=jnp.float32), 0.0).astype(jnp.bfloat16)
        grad_up = jnp.dot(lowered_program.T, gradient_list, preferred_element_type=jnp.float32)
        grad_down = jnp.dot(input_rows.T, raised_error, preferred_element_type=jnp.float32)
        pre_up = precondition(grad_up, expanding_running_average, expanding_running_variance)
        pre_down = precondition(grad_down, shrinking_running_average, shrinking_running_variance)
        part_up = jnp.dot(up_rank_projector.T, jnp.dot(pre_up, up_width_projector, precision=high), precision=high)
        part_down = jnp.dot(down_rank_projector.T, jnp.dot(pre_down.T, down_width_projector, precision=high), precision=high)
        raw = jnp.concatenate([part_up.reshape(-1), part_down.reshape(-1)])
        return raw / jnp.sqrt(jnp.mean(raw * raw) + 1e-06)
    return lax.map(one_example, (activations, output_gradient_rows, lengths))
```

```python
import functools

import jax
import jax.numpy as jnp
from jax import lax
from jax.experimental import pallas as pl
from jax.experimental.pallas import tpu as pltpu
from jax.sharding import Mesh, PartitionSpec as P

BLK = 128
FOOT = 16
RES = 128.0
TOP = 32767.0
MIB = 1024 * 1024
VMEM = pltpu.VMEM
SMEM = pltpu.SMEM
F32 = jnp.float32
BF16 = jnp.bfloat16
I16 = jnp.int16
I32 = jnp.int32


def scale_code(peak):
    return jnp.ceil(jnp.log(jnp.maximum(peak, 1e-30)) * (RES / 0.6931471805599453)) + 1.0


def scale_of(code):
    return jnp.exp2(code * (1.0 / RES))


def encode(x):
    code = scale_code(jnp.max(jnp.abs(x), axis=0, keepdims=True))
    q = jnp.round(x * (TOP / scale_of(code)))
    return q.astype(I32).astype(I16), code


def partial_kernel(nblk, tab, base, w, a_hbm, g_hbm, q, abuf, gbuf, codes, sems):
    first = base[0]

    def copies(k):
        e, t = tab[0, first + k], pl.multiple_of(tab[1, first + k], BLK)
        return (
            pltpu.make_async_copy(a_hbm.at[e, pl.ds(t, BLK)], abuf.at[k], sems.at[0, k]),
            pltpu.make_async_copy(g_hbm.at[e, pl.ds(t, BLK)], gbuf.at[k], sems.at[1, k]),
        )

    for k in range(nblk):
        for c in copies(k):
            c.start()
    rank = w.shape[1] // 2
    ws = w[:, :rank, :].reshape(-1, w.shape[2])
    we = w[:, rank:, :].reshape(-1, w.shape[2])
    codes[...] = jnp.zeros_like(codes)
    nt = (((1,), (1,)), ((), ()))
    for k in range(nblk):
        for c in copies(k):
            c.wait()
        live = lax.broadcasted_iota(I32, (BLK, 1), 0) < tab[2, first + k]
        for i, (buf, weight) in enumerate(((abuf, ws), (gbuf, we))):
            x = lax.dot_general(buf[k], weight, nt, preferred_element_type=F32)
            x = jnp.where(live, x, 0.0)
            coded, code = encode(x)
            q[k * BLK : (k + 1) * BLK, i * 128 : (i + 1) * 128] = coded
            codes[k : k + 1, i * 128 : (i + 1) * 128] = code
    q[nblk * BLK :, :] = codes[...].astype(I32).astype(I16)


def partial_piece(tab, base, w, a, g, nblk):
    rows = nblk * BLK
    return pl.pallas_call(
        functools.partial(partial_kernel, nblk),
        out_shape=jax.ShapeDtypeStruct((rows + FOOT, 256), I16),
        in_specs=[
            pl.BlockSpec(memory_space=SMEM),
            pl.BlockSpec(memory_space=SMEM),
            pl.BlockSpec(memory_space=VMEM),
            pl.BlockSpec(memory_space=pl.ANY),
            pl.BlockSpec(memory_space=pl.ANY),
        ],
        out_specs=pl.BlockSpec(memory_space=VMEM),
        scratch_shapes=[
            VMEM((nblk, BLK, 512), BF16),
            VMEM((nblk, BLK, 512), BF16),
            VMEM((FOOT, 256), F32),
            pltpu.SemaphoreType.DMA((2, nblk)),
        ],
        compiler_params=pltpu.CompilerParams(vmem_limit_bytes=16 * MIB),
        cost_estimate=pl.CostEstimate(
            flops=4 * rows * 512 * 128, bytes_accessed=rows * (2048 + 512), transcendentals=0
        ),
    )(tab, base, w, a, g)


def scales_of(refs, rows, count):
    return [scale_of(r[rows:, :].astype(I32).astype(F32)) * (1.0 / TOP) for r in refs]


def value(ref, start, n):
    return ref[pl.ds(start, n), :].astype(I32).astype(F32)


def middle_kernel(rows, sub, step, order, q0, q1, q2, q3, r0, r1, r2, r3, scales, codes):
    refs, outs = (q0, q1, q2, q3), (r0, r1, r2, r3)
    for i, s in enumerate(scales_of(refs, rows, rows // BLK)):
        scales[i] = s
    for s in range(4):
        codes[...] = jnp.zeros_like(codes)
        begin = order[s] * sub
        for j in range(sub // step):
            at = pl.multiple_of(begin + j * step, step)
            blk = at // BLK
            total = None
            for i, r in enumerate(refs):
                v = value(r, at, step) * scales[i, pl.ds(blk, 1), :]
                total = v if total is None else total + v
            coded, code = encode(total)
            outs[s][j * step : (j + 1) * step, :] = coded
            codes[j : j + 1, :] = code
        outs[s][sub:, :] = codes[...].astype(I32).astype(I16)


def middle_sum(order, pieces, rows, sub, step):
    return pl.pallas_call(
        functools.partial(middle_kernel, rows, sub, step),
        out_shape=[jax.ShapeDtypeStruct((sub + FOOT, 256), I16)] * 4,
        in_specs=[pl.BlockSpec(memory_space=SMEM)] + [pl.BlockSpec(memory_space=VMEM)] * 4,
        out_specs=[pl.BlockSpec(memory_space=VMEM)] * 4,
        scratch_shapes=[VMEM((4, FOOT, 256), F32), VMEM((FOOT, 256), F32)],
        compiler_params=pltpu.CompilerParams(vmem_limit_bytes=16 * MIB),
        cost_estimate=pl.CostEstimate(
            flops=rows * 256 * 8, bytes_accessed=rows * 256 * 10, transcendentals=0
        ),
    )(order, *pieces)


def last_kernel(sub, step, r0, r1, r2, r3, out):
    refs = (r0, r1, r2, r3)
    scales = scales_of(refs, sub, sub // step)
    for j in range(sub // step):
        total = None
        for i, r in enumerate(refs):
            v = value(r, j * step, step) * scales[i][j : j + 1, :]
            total = v if total is None else total + v
        out[j * step : (j + 1) * step, :] = total.astype(BF16)


def last_sum(pieces, sub, step):
    return pl.pallas_call(
        functools.partial(last_kernel, sub, step),
        out_shape=jax.ShapeDtypeStruct((sub, 256), BF16),
        in_specs=[pl.BlockSpec(memory_space=VMEM)] * 4,
        out_specs=pl.BlockSpec(memory_space=VMEM),
        compiler_params=pltpu.CompilerParams(vmem_limit_bytes=8 * MIB),
        cost_estimate=pl.CostEstimate(
            flops=sub * 256 * 8, bytes_accessed=sub * 256 * 10, transcendentals=0
        ),
    )(*pieces)


def precondition(grad, first, second):
    top = 0.9 * first + 0.1 * grad
    return top / (jnp.sqrt(0.999 * second + 0.001 * grad * grad) + 1e-08)


def grads_kernel(nb, sub, tab, heads, place, *refs):
    pieces = refs[:8]
    a_hbm, g_hbm, moments, urp, uwp, dwp, drp, out, lr, abuf, gbuf, up, down, sems, lsems = refs[8:]

    def copies(b):
        e, t = tab[0, b], pl.multiple_of(tab[1, b], BLK)
        return (
            pltpu.make_async_copy(a_hbm.at[e, pl.ds(t, BLK)], abuf.at[b], sems.at[0, b]),
            pltpu.make_async_copy(g_hbm.at[e, pl.ds(t, BLK)], gbuf.at[b], sems.at[1, b]),
        )

    spread = []
    for p, piece in enumerate(pieces):
        for s in range(4):
            at = pl.multiple_of(place[p * 4 + s] * sub, 32)
            spread.append(
                pltpu.make_async_copy(
                    piece.at[pl.ds(s * sub, sub)], lr.at[pl.ds(at, sub)], lsems.at[p * 4 + s]
                )
            )
    for c in spread:
        c.start()

    def begin(b, carry):
        for c in copies(b):
            c.start()
        return carry

    total = heads[6]
    lax.fori_loop(0, total, begin, 0)
    for c in spread:
        c.wait()
    tn = (((0,), (0,)), ((), ()))
    high = lax.Precision.HIGHEST
    rank = moments.shape[1] // 4

    def moment(i):
        return moments[:, i * rank : (i + 1) * rank, :].reshape(-1, moments.shape[2])

    for e in range(6):
        up[...] = jnp.zeros_like(up)
        down[...] = jnp.zeros_like(down)

        def step(b, carry):
            for c in copies(b):
                c.wait()
            rows = pl.ds(pl.multiple_of(b * BLK, BLK), BLK)
            up[...] += lax.dot_general(lr[rows, :128], gbuf[b], tn, preferred_element_type=F32)
            down[...] += lax.dot_general(lr[rows, 128:], abuf[b], tn, preferred_element_type=F32)
            return carry

        lax.fori_loop(heads[e], heads[e + 1], step, 0)
        for i, (grad, width, side) in enumerate(((up, uwp, urp), (down, dwp, drp))):
            pre = precondition(grad[...], moment(2 * i), moment(2 * i + 1))
            wide = jnp.dot(pre, width[...], precision=high, preferred_element_type=F32)
            if i == 0:
                part = lax.dot_general(side[...], wide, tn, precision=high, preferred_element_type=F32)
            else:
                part = lax.dot_general(side[...], wide, tn, precision=high, preferred_element_type=F32)
            out[e, i * 64 : (i + 1) * 64, :] = part


def grads(tab, heads, place, pieces, a, g, moments, urp, uwp, dwp, drp, nb, sub):
    return pl.pallas_call(
        functools.partial(grads_kernel, nb, sub),
        out_shape=jax.ShapeDtypeStruct((6, 128, 64), F32),
        in_specs=[pl.BlockSpec(memory_space=SMEM)] * 3
        + [pl.BlockSpec(memory_space=pl.ANY)] * 10
        + [pl.BlockSpec(memory_space=VMEM)] * 5,
        out_specs=pl.BlockSpec(memory_space=VMEM),
        scratch_shapes=[
            VMEM((nb * BLK, 256), BF16),
            VMEM((nb, BLK, 512), BF16),
            VMEM((nb, BLK, 512), BF16),
            VMEM((128, 512), F32),
            VMEM((128, 512), F32),
            pltpu.SemaphoreType.DMA((2, nb)),
            pltpu.SemaphoreType.DMA((32,)),
        ],
        compiler_params=pltpu.CompilerParams(vmem_limit_bytes=48 * MIB),
        cost_estimate=pl.CostEstimate(
            flops=4 * nb * BLK * 512 * 128, bytes_accessed=nb * BLK * 2560, transcendentals=0
        ),
    )(tab, heads, place, *pieces, a, g, moments, urp, uwp, dwp, drp)


def block_table(lengths, nb):
    counts = (lengths + (BLK - 1)) // BLK
    ends = jnp.cumsum(counts)
    heads = jnp.concatenate([jnp.zeros((1,), I32), ends]).astype(I32)
    b = jnp.arange(nb, dtype=I32)
    e = jnp.sum((b[:, None] >= ends[None, :]).astype(I32), axis=1)
    inside = e < lengths.shape[0]
    e = jnp.minimum(e, lengths.shape[0] - 1)
    pick = (e[:, None] == jnp.arange(lengths.shape[0], dtype=I32)[None, :]).astype(I32)
    t = jnp.where(inside, (b - jnp.sum(pick * heads[None, :-1], axis=1)) * BLK, 0)
    rows = jnp.where(inside, jnp.clip(jnp.sum(pick * lengths[None, :], axis=1) - t, 0, BLK), 0)
    return jnp.stack([e, t, rows]).astype(I32), heads


def shift_of(n, s):
    return [(i, (i + s) % n) for i in range(n)]


def features(nb, lengths, w, moments, a, g, urp, uwp, dwp, drp):
    tokens = nb * BLK
    rows, sub, step, per = tokens // 8, tokens // 32, 32, nb // 8
    tab, heads = block_table(lengths, nb)
    here = {"y": lax.axis_index("y").astype(I32), "z": lax.axis_index("z").astype(I32)}
    halves = (("y", "z"), ("z", "y"))

    def send(x, axis, s):
        return lax.ppermute(x, axis, shift_of(4, s))

    coded = {}
    for s in (2, 1, 3, 0):
        for h, (first, _) in enumerate(halves):
            base = h * (nb // 2) + ((here[first] + s) % 4) * per
            coded[h, s] = partial_piece(tab, base.reshape(1), w, a, g, per)
    got = {(h, s): coded[h, s] if s == 0 else send(coded[h, s], halves[h][0], s) for h, s in coded}
    shifts = jnp.arange(4, dtype=I32)
    mids = [
        middle_sum((here[second] + shifts) % 4, [got[h, s] for s in range(4)], rows, sub, step)
        for h, (_, second) in enumerate(halves)
    ]
    sums = []
    for h, (_, second) in enumerate(halves):
        arrived = [mids[h][s] if s == 0 else send(mids[h][s], second, s) for s in range(4)]
        sums.append(last_sum(arrived, sub, step))
    pieces, place = [], []
    for h, (first, second) in enumerate(halves):
        block = jnp.concatenate(
            [sums[h] if s == 0 else send(sums[h], second, s) for s in range(4)], axis=0
        )
        for s in range(4):
            pieces.append(block if s == 0 else send(block, first, s))
            owner = (here[first] - s) % 4
            place.append(h * 16 + owner * 4 + (here[second] - shifts) % 4)
    place = jnp.concatenate(place).astype(I32)
    return grads(tab, heads, place, pieces, a, g, moments, urp, uwp, dwp, drp, nb, sub)


def body(a, g, lengths, sf, ef, sra, srv, era, erv, urp, uwp, dwp, drp):
    dp, param = ("x", "core"), ("z", "y")
    w = lax.all_gather(jnp.concatenate([sf.T, ef], axis=0), dp, axis=0)
    moments = lax.all_gather(jnp.concatenate([era, erv, sra.T, srv.T], axis=0), dp, axis=0)
    nb = a.shape[0] * a.shape[1] // BLK
    part = features(nb, lengths, w, moments, a, g, urp, uwp, dwp, drp)
    owned = jnp.swapaxes(part.reshape(6, 16, 8, 64), 0, 1)
    raw = jnp.sum(lax.all_to_all(owned, param, 0, 0, tiled=True), axis=0)
    square = lax.psum(lax.psum(jnp.sum(raw * raw, axis=(1, 2)), "y"), "z")
    scale = lax.rsqrt(square / 8192.0 + 1e-06)
    return (raw * scale[:, None, None]).reshape(6, 512)


def solution(mesh):
    grid = Mesh(mesh.devices.reshape(4, 2, 4, 4), ("x", "core", "z", "y"))
    dp, param = ("x", "core"), ("z", "y")
    in_specs = (
        P(dp, None, param),
        P(dp, None, param),
        P(dp),
        P(param, dp),
        P(dp, param),
        P(param, dp),
        P(param, dp),
        P(dp, param),
        P(dp, param),
        P(),
        P(param, None),
        P(param, None),
        P(),
    )
    return jax.shard_map(body, mesh=grid, in_specs=in_specs, out_specs=P(dp, param), check_vma=False)
```

```python
import functools

import jax
import jax.numpy as jnp
from jax import lax
from jax.experimental import pallas as pl
from jax.experimental.pallas import tpu as pltpu
from jax.sharding import Mesh, PartitionSpec as P

BLK = 128
FOOT = 32
RES = 128.0
TOP = 32767.0
MIB = 1024 * 1024
VMEM = pltpu.VMEM
SMEM = pltpu.SMEM
F32 = jnp.float32
BF16 = jnp.bfloat16
I16 = jnp.int16
I32 = jnp.int32


def scale_code(peak):
    return jnp.ceil(jnp.log(jnp.maximum(peak, 1e-30)) * (RES / 0.6931471805599453)) + 1.0


def scale_of(code):
    return jnp.exp2(code * (1.0 / RES))


def encode(x):
    code = scale_code(jnp.max(jnp.abs(x), axis=0, keepdims=True))
    q = jnp.round(x * (TOP / scale_of(code)))
    return q.astype(I32).astype(I16), code


def position():
    y, z = lax.axis_index("y").astype(I32), lax.axis_index("z").astype(I32)
    zero = lax.axis_index("core") == 0
    return jnp.where(zero, y, z), jnp.where(zero, z, y)


def block_counts(lens):
    return [(lens[e] + (BLK - 1)) // BLK for e in range(lens.shape[0])]


def locate(b, lens):
    n = lens.shape[0]
    start, e, end = jnp.int32(0), jnp.int32(0), jnp.int32(0)
    for count in block_counts(lens):
        end = end + count
        past = b >= end
        start = jnp.where(past, end, start)
        e = jnp.where(past, e + 1, e)
    inside = e < n
    e = jnp.minimum(e, n - 1)
    t = jnp.where(inside, (b - start) * BLK, 0)
    return e, t, jnp.where(inside, jnp.clip(lens[e] - t, 0, BLK), 0)


def dp_place():
    return lax.axis_index("x").astype(I32) * 2 + lax.axis_index("core").astype(I32)


def ring_of(x):
    n = 8
    others = [
        lax.ppermute(x, ("x", "core"), [(i, (i + s) % n) for i in range(n)]) for s in range(1, n)
    ]
    return [x] + others


def load_kernel(a_hbm, g_hbm, a, g, sems):
    copies = [
        pltpu.make_async_copy(a_hbm, a, sems.at[0]),
        pltpu.make_async_copy(g_hbm, g, sems.at[1]),
    ]
    for c in copies:
        c.start()
    for c in copies:
        c.wait()


def load(a, g):
    return pl.pallas_call(
        load_kernel,
        out_shape=[VMEM(a.shape, a.dtype), VMEM(g.shape, g.dtype)],
        in_specs=[pl.BlockSpec(memory_space=pl.ANY)] * 2,
        out_specs=[pl.BlockSpec(memory_space=VMEM)] * 2,
        scratch_shapes=[pltpu.SemaphoreType.DMA((2,))],
        compiler_params=pltpu.CompilerParams(vmem_limit_bytes=24 * MIB),
        cost_estimate=pl.CostEstimate(flops=0, bytes_accessed=a.size * 4, transcendentals=0),
    )(a, g)


def turn_kernel(*refs):
    parts, (w, flat) = refs[:8], refs[8:]
    me = dp_place()
    rank = parts[0].shape[1]
    for s, part in enumerate(parts):
        at = pl.ds(pl.multiple_of((me - s) % 8 * rank, rank), rank)
        for i in range(2):
            flat[i, at, :] = part[i]
    for i in range(2):
        w[i] = flat[i].T


def turn(parts):
    _, rank, width = parts[0].shape
    return pl.pallas_call(
        turn_kernel,
        out_shape=jax.ShapeDtypeStruct((2, width, 8 * rank), BF16),
        in_specs=[pl.BlockSpec(memory_space=VMEM)] * 8,
        out_specs=pl.BlockSpec(memory_space=VMEM),
        scratch_shapes=[VMEM((2, 8 * rank, width), BF16)],
        compiler_params=pltpu.CompilerParams(vmem_limit_bytes=4 * MIB),
    )(*parts)


def foot(ref, start, codes, count):
    rows = [codes[k] for k in range(count)]
    rows.append(jnp.zeros((FOOT - count, 256), F32))
    ref[start:, :] = jnp.concatenate(rows, axis=0).astype(I32).astype(I16)


def partial_kernel(nblk, s, lens, w, a, g, q, codes):
    first = (position()[0] + s) % 4 * nblk

    def block(k, carry):
        e, t, count = locate(first + k, lens)
        t = pl.multiple_of(t, BLK)
        at = pl.ds(pl.multiple_of(k * BLK, BLK), BLK)
        live = lax.broadcasted_iota(I32, (BLK, 128), 0) < count
        for i, rows in enumerate((a, g)):
            x = jnp.dot(rows[e, pl.ds(t, BLK), :], w[i], preferred_element_type=F32)
            x = jnp.where(live, x, 0.0)
            coded, code = encode(x)
            q[at, i * 128 : (i + 1) * 128] = coded
            codes[k, :, i * 128 : (i + 1) * 128] = code
        return carry

    lax.fori_loop(0, nblk, block, 0, unroll=4)
    foot(q, nblk * BLK, codes, nblk)


def partial_piece(lens, w, a, g, nblk, s):
    rows = nblk * BLK
    return pl.pallas_call(
        functools.partial(partial_kernel, nblk, s),
        out_shape=jax.ShapeDtypeStruct((rows + FOOT, 256), I16),
        in_specs=[pl.BlockSpec(memory_space=SMEM)] + [pl.BlockSpec(memory_space=VMEM)] * 3,
        out_specs=pl.BlockSpec(memory_space=VMEM),
        scratch_shapes=[VMEM((FOOT, 1, 256), F32)],
        compiler_params=pltpu.CompilerParams(vmem_limit_bytes=6 * MIB),
        cost_estimate=pl.CostEstimate(
            flops=16 * rows * 512 * 128, bytes_accessed=rows * 2048, transcendentals=0
        ),
    )(lens, w, a, g)


def scales_of(refs, rows, count):
    return [scale_of(r[rows:, :].astype(I32).astype(F32)) * (1.0 / TOP) for r in refs]


def value(ref, start, n):
    return ref[pl.ds(start, n), :].astype(I32).astype(F32)


def middle_kernel(rows, sub, step, which, q0, q1, q2, q3, *rest):
    refs, outs, (scales, codes) = (q0, q1, q2, q3), rest[:-2], rest[-2:]
    two = position()[1]
    for i, s in enumerate(scales_of(refs, rows, rows // BLK)):
        scales[i] = s
    for s, out in zip(which, outs):
        begin = (two + s) % 4 * sub

        def some(j, carry, out=out, begin=begin):
            at = pl.multiple_of(begin + j * step, step)
            total = None
            for i, r in enumerate(refs):
                v = value(r, at, step) * scales[i, pl.ds(at // BLK, 1), :]
                total = v if total is None else total + v
            coded, code = encode(total)
            out[pl.ds(pl.multiple_of(j * step, step), step), :] = coded
            codes[j] = code
            return carry

        lax.fori_loop(0, sub // step, some, 0, unroll=4)
        foot(out, sub, codes, sub // step)


def middle_sum(pieces, rows, sub, step, which):
    return pl.pallas_call(
        functools.partial(middle_kernel, rows, sub, step, which),
        out_shape=[jax.ShapeDtypeStruct((sub + FOOT, 256), I16)] * len(which),
        in_specs=[pl.BlockSpec(memory_space=VMEM)] * 4,
        out_specs=[pl.BlockSpec(memory_space=VMEM)] * len(which),
        scratch_shapes=[VMEM((4, FOOT, 256), F32), VMEM((FOOT, 1, 256), F32)],
        compiler_params=pltpu.CompilerParams(vmem_limit_bytes=10 * MIB),
        cost_estimate=pl.CostEstimate(
            flops=rows * 64 * 8 * len(which), bytes_accessed=rows * 256 * 2, transcendentals=0
        ),
    )(*pieces)


def last_kernel(sub, step, r0, r1, r2, r3, out):
    refs = (r0, r1, r2, r3)
    scales = scales_of(refs, sub, sub // step)
    for j in range(sub // step):
        total = None
        for i, r in enumerate(refs):
            v = value(r, j * step, step) * scales[i][j : j + 1, :]
            total = v if total is None else total + v
        out[j * step : (j + 1) * step, :] = total.astype(BF16)


def last_sum(pieces, sub, step):
    return pl.pallas_call(
        functools.partial(last_kernel, sub, step),
        out_shape=jax.ShapeDtypeStruct((sub, 256), BF16),
        in_specs=[pl.BlockSpec(memory_space=VMEM)] * 4,
        out_specs=pl.BlockSpec(memory_space=VMEM),
        compiler_params=pltpu.CompilerParams(vmem_limit_bytes=6 * MIB),
        cost_estimate=pl.CostEstimate(
            flops=sub * 256 * 8, bytes_accessed=sub * 256 * 10, transcendentals=0
        ),
    )(*pieces)


def precondition(grad, first, second):
    top = 0.9 * first + 0.1 * grad
    return top / (jnp.sqrt(0.999 * second + 0.001 * grad * grad) + 1e-08)


def join_kernel(r0, r1, r2, r3, out):
    two = position()[1]
    for s, r in enumerate((r0, r1, r2, r3)):
        out[(two - s) % 4] = r[...]


def join(parts):
    sub = parts[0].shape[0]
    return pl.pallas_call(
        join_kernel,
        out_shape=jax.ShapeDtypeStruct((4, sub, 256), BF16),
        in_specs=[pl.BlockSpec(memory_space=VMEM)] * 4,
        out_specs=pl.BlockSpec(memory_space=VMEM),
        compiler_params=pltpu.CompilerParams(vmem_limit_bytes=8 * MIB),
    )(*parts).reshape(4 * sub, 256)


def gather_sums(which, nblk, lens, pieces, a, g, up, down):
    tn = (((0,), (0,)), ((), ()))
    one = position()[0]
    for s, piece in zip(which, pieces):
        low = (one - s) % 4 * nblk

        def example(e, begin, piece=piece, low=low):
            count = (lens[e] + (BLK - 1)) // BLK
            first = jnp.clip(begin - low, 0, nblk)
            some = jnp.clip(begin + count - low, 0, nblk) - first
            skip = jnp.maximum(low - begin, 0)

            def add(b, n):
                packed = pl.ds(pl.multiple_of((first + b) * BLK, BLK), n * BLK)
                rows = pl.ds(pl.multiple_of((skip + b) * BLK, BLK), n * BLK)
                up[e] += lax.dot_general(
                    piece[packed, :128], g[e, rows, :], tn, preferred_element_type=F32
                )
                down[e] += lax.dot_general(
                    piece[packed, 128:], a[e, rows, :], tn, preferred_element_type=F32
                )

            for n in (16, 8, 4, 2, 1):

                @pl.when((some // n) % 2 == 1)
                def _(n=n):
                    add(some // (2 * n) * (2 * n), n)

            return begin + count

        lax.fori_loop(0, 6, example, jnp.int32(0))


def early_kernel(which, nblk, lens, *refs):
    n = len(which)
    a, g, up, down = refs[n:]
    up[...] = jnp.zeros_like(up)
    down[...] = jnp.zeros_like(down)
    gather_sums(which, nblk, lens, refs[:n], a, g, up, down)


def early_grads(which, nblk, lens, pieces, a, g):
    grad = jax.ShapeDtypeStruct((6, 128, 512), F32)
    return pl.pallas_call(
        functools.partial(early_kernel, which, nblk),
        out_shape=[grad, grad],
        in_specs=[pl.BlockSpec(memory_space=SMEM)]
        + [pl.BlockSpec(memory_space=VMEM)] * (len(which) + 2),
        out_specs=[pl.BlockSpec(memory_space=VMEM)] * 2,
        compiler_params=pltpu.CompilerParams(vmem_limit_bytes=6 * MIB),
        cost_estimate=pl.CostEstimate(
            flops=4 * nblk * len(which) * BLK * 512 * 128,
            bytes_accessed=nblk * len(which) * BLK * 512,
            transcendentals=0,
        ),
    )(lens, *pieces, a, g)


def final_kernel(which, nblk, lens, *refs):
    n = len(which)
    a, g, up0, down0 = refs[n : n + 4]
    parts = refs[n + 4 : n + 12]
    urp, uwp, dwp, drp, out, up, down, moments = refs[n + 12 :]
    nt = (((1,), (1,)), ((), ()))
    high = lax.Precision.HIGHEST
    me = dp_place()
    rank = parts[0].shape[0] // 4
    for s, part in enumerate(parts):
        at = pl.ds(pl.multiple_of((me - s) % 8 * rank, rank), rank)
        for i in range(4):
            moments[i, at, :] = part[i * rank : (i + 1) * rank, :]
    up[...] = up0[...]
    down[...] = down0[...]
    gather_sums(which, nblk, lens, refs[:n], a, g, up, down)

    def example(e, carry):
        for i, (grad, width, side) in enumerate(((up, uwp, urp), (down, dwp, drp))):
            pre = precondition(grad[e], moments[2 * i], moments[2 * i + 1])
            wide = lax.dot_general(
                pre, width[...], nt, precision=high, preferred_element_type=F32
            )
            out[e, i * 64 : (i + 1) * 64, :] = jnp.dot(
                side[...], wide, precision=high, preferred_element_type=F32
            )
        return carry

    lax.fori_loop(0, 6, example, 0)


def final_grads(which, nblk, lens, pieces, a, g, up, down, moments, *projectors):
    return pl.pallas_call(
        functools.partial(final_kernel, which, nblk),
        out_shape=jax.ShapeDtypeStruct((6, 128, 64), F32),
        in_specs=[pl.BlockSpec(memory_space=SMEM)]
        + [pl.BlockSpec(memory_space=VMEM)] * (len(which) + 16),
        out_specs=pl.BlockSpec(memory_space=VMEM),
        scratch_shapes=[
            VMEM((6, 128, 512), F32),
            VMEM((6, 128, 512), F32),
            VMEM((4, 128, 512), F32),
        ],
        compiler_params=pltpu.CompilerParams(vmem_limit_bytes=10 * MIB),
        cost_estimate=pl.CostEstimate(
            flops=4 * nblk * len(which) * BLK * 512 * 128,
            bytes_accessed=nblk * len(which) * BLK * 512,
            transcendentals=0,
        ),
    )(lens, *pieces, a, g, up, down, *moments, *projectors)


def shifts(first, s):
    pairs = []
    for core in range(2):
        for z in range(4):
            for y in range(4):
                along_y = (core == 0) == first
                to = (z, (y + s) % 4) if along_y else ((z + s) % 4, y)
                pairs.append((core * 16 + z * 4 + y, core * 16 + to[0] * 4 + to[1]))
    return pairs


def send(x, first, s):
    return x if s == 0 else lax.ppermute(x, ("core", "z", "y"), shifts(first, s))


def features(nb, lens, w, moments, a, g, projectors):
    rows, sub, step, per = nb * BLK // 4, nb * BLK // 16, 32, nb // 4
    got = [None] * 4
    for s in (2, 1, 3, 0):
        got[s] = send(partial_piece(lens, w, a, g, per, s), True, s)
    got[0], moments = lax.optimization_barrier((got[0], moments))
    ring = ring_of(moments)
    back = [None] * 4
    for which in ((2,), (1, 3, 0)):
        for s, mid in zip(which, middle_sum(got, rows, sub, step, which)):
            back[s] = send(mid, False, s)
    own = last_sum(back, sub, step)
    piece = join([send(own, False, s) for s in range(4)])
    pieces = {s: send(piece, True, s) for s in (0, 1, 3, 2)}
    soon, late = (0, 1, 3), (2,)
    up, down = early_grads(soon, per, lens, [pieces[s] for s in soon], a, g)
    return final_grads(
        late, per, lens, [pieces[s] for s in late], a, g, up, down, ring, *projectors
    )


def share(x, axes, n):
    return lax.all_to_all(jnp.broadcast_to(x[None], (n,) + x.shape), axes, 0, 0, tiled=True)


def body(a, g, lengths, sf, ef, sra, srv, era, erv, urp, uwp, dwp, drp):
    param = ("z", "y")
    w = turn(ring_of(jnp.stack([sf.T, ef])))
    a, g = load(a, g)
    moments = jnp.concatenate([era, erv, sra.T, srv.T], axis=0)
    nb = a.shape[0] * a.shape[1] // BLK
    part = features(nb, lengths, w, moments, a, g, (urp.T, uwp.T, dwp.T, drp.T))
    owned = jnp.swapaxes(part.reshape(6, 16, 8, 64), 0, 1)
    raw = jnp.sum(lax.all_to_all(owned, param, 0, 0, tiled=True), axis=0)
    square = jnp.sum(raw * raw, axis=(1, 2))
    square = share(jnp.broadcast_to(square[:, None], (6, 128)), param, 16)
    scale = lax.rsqrt(jnp.sum(square, axis=0)[:, 0] / 8192.0 + 1e-06)
    return (raw * scale[:, None, None]).reshape(6, 512)


def solution(mesh):
    grid = Mesh(mesh.devices.reshape(4, 2, 4, 4), ("x", "core", "z", "y"))
    dp, param = ("x", "core"), ("z", "y")
    in_specs = (
        P(dp, None, param),
        P(dp, None, param),
        P(dp),
        P(param, dp),
        P(dp, param),
        P(param, dp),
        P(param, dp),
        P(dp, param),
        P(dp, param),
        P(),
        P(param, None),
        P(param, None),
        P(),
    )
    return jax.shard_map(body, mesh=grid, in_specs=in_specs, out_specs=P(dp, param), check_vma=False)
```

```python
import functools

import jax
import jax.numpy as jnp
from jax import lax
from jax.experimental import pallas as pl
from jax.experimental.pallas import tpu as pltpu
from jax.sharding import Mesh, PartitionSpec as P

BLK = 128
FOOT = 32
RES = 128.0
TOP = 32767.0
MIB = 1024 * 1024
VMEM = pltpu.VMEM
SMEM = pltpu.SMEM
F32 = jnp.float32
BF16 = jnp.bfloat16
I16 = jnp.int16
I32 = jnp.int32


def scale_code(peak):
    return jnp.ceil(jnp.log(jnp.maximum(peak, 1e-30)) * (RES / 0.6931471805599453)) + 1.0


def scale_of(code):
    return jnp.exp2(code * (1.0 / RES))


def encode(x):
    code = scale_code(jnp.max(jnp.abs(x), axis=0, keepdims=True))
    q = jnp.round(x * (TOP / scale_of(code)))
    return q.astype(I32).astype(I16), code


def position():
    y, z = lax.axis_index("y").astype(I32), lax.axis_index("z").astype(I32)
    zero = lax.axis_index("core") == 0
    return jnp.where(zero, y, z), jnp.where(zero, z, y)


def block_counts(lens):
    return [(lens[e] + (BLK - 1)) // BLK for e in range(lens.shape[0])]


def locate(b, lens):
    n = lens.shape[0]
    start, e, end = jnp.int32(0), jnp.int32(0), jnp.int32(0)
    for count in block_counts(lens):
        end = end + count
        past = b >= end
        start = jnp.where(past, end, start)
        e = jnp.where(past, e + 1, e)
    inside = e < n
    e = jnp.minimum(e, n - 1)
    t = jnp.where(inside, (b - start) * BLK, 0)
    return e, t, jnp.where(inside, jnp.clip(lens[e] - t, 0, BLK), 0)


def dp_place():
    return lax.axis_index("x").astype(I32) * 2 + lax.axis_index("core").astype(I32)


def ring_of(x):
    n = 8
    others = [
        lax.ppermute(x, ("x", "core"), [(i, (i + s) % n) for i in range(n)]) for s in range(1, n)
    ]
    return [x] + others


def load_kernel(a_hbm, g_hbm, a, g, sems):
    copies = [
        pltpu.make_async_copy(a_hbm, a, sems.at[0]),
        pltpu.make_async_copy(g_hbm, g, sems.at[1]),
    ]
    for c in copies:
        c.start()
    for c in copies:
        c.wait()


def load(a, g):
    return pl.pallas_call(
        load_kernel,
        out_shape=[VMEM(a.shape, a.dtype), VMEM(g.shape, g.dtype)],
        in_specs=[pl.BlockSpec(memory_space=pl.ANY)] * 2,
        out_specs=[pl.BlockSpec(memory_space=VMEM)] * 2,
        scratch_shapes=[pltpu.SemaphoreType.DMA((2,))],
        compiler_params=pltpu.CompilerParams(vmem_limit_bytes=24 * MIB),
        cost_estimate=pl.CostEstimate(flops=0, bytes_accessed=a.size * 4, transcendentals=0),
    )(a, g)


def turn_kernel(*refs):
    parts, (w, flat) = refs[:8], refs[8:]
    me = dp_place()
    rank = parts[0].shape[1]
    for s, part in enumerate(parts):
        at = pl.ds(pl.multiple_of((me - s) % 8 * rank, rank), rank)
        for i in range(2):
            flat[i, at, :] = part[i]
    for i in range(2):
        w[i] = flat[i].T


def turn(parts):
    _, rank, width = parts[0].shape
    return pl.pallas_call(
        turn_kernel,
        out_shape=jax.ShapeDtypeStruct((2, width, 8 * rank), BF16),
        in_specs=[pl.BlockSpec(memory_space=VMEM)] * 8,
        out_specs=pl.BlockSpec(memory_space=VMEM),
        scratch_shapes=[VMEM((2, 8 * rank, width), BF16)],
        compiler_params=pltpu.CompilerParams(vmem_limit_bytes=2 * MIB),
    )(*parts)


def foot(ref, start, codes, count):
    rows = [codes[k] for k in range(count)]
    rows.append(jnp.zeros((FOOT - count, 256), F32))
    ref[start:, :] = jnp.concatenate(rows, axis=0).astype(I32).astype(I16)


def partial_kernel(nblk, s, lens, w, a, g, q, codes):
    first = (position()[0] + s) % 4 * nblk

    def block(k, carry):
        e, t, count = locate(first + k, lens)
        t = pl.multiple_of(t, BLK)
        at = pl.ds(pl.multiple_of(k * BLK, BLK), BLK)
        live = lax.broadcasted_iota(I32, (BLK, 128), 0) < count
        for i, rows in enumerate((a, g)):
            x = jnp.dot(rows[e, pl.ds(t, BLK), :], w[i], preferred_element_type=F32)
            x = jnp.where(live, x, 0.0)
            coded, code = encode(x)
            q[at, i * 128 : (i + 1) * 128] = coded
            codes[k, :, i * 128 : (i + 1) * 128] = code
        return carry

    lax.fori_loop(0, nblk, block, 0, unroll=2)
    foot(q, nblk * BLK, codes, nblk)


def partial_piece(lens, w, a, g, nblk, s):
    rows = nblk * BLK
    return pl.pallas_call(
        functools.partial(partial_kernel, nblk, s),
        out_shape=jax.ShapeDtypeStruct((rows + FOOT, 256), I16),
        in_specs=[pl.BlockSpec(memory_space=SMEM)] + [pl.BlockSpec(memory_space=VMEM)] * 3,
        out_specs=pl.BlockSpec(memory_space=VMEM),
        scratch_shapes=[VMEM((FOOT, 1, 256), F32)],
        compiler_params=pltpu.CompilerParams(vmem_limit_bytes=2 * MIB),
        cost_estimate=pl.CostEstimate(
            flops=1000, bytes_accessed=1000, transcendentals=0
        ),
    )(lens, w, a, g)


def far_kernel(nblk, chunk, s, lens, w, a_hbm, g_hbm, q, a, g, codes, sems):
    first = (position()[0] + s) % 4 * nblk

    def copies(k):
        e, t, _ = locate(first + k, lens)
        here = pl.ds(pl.multiple_of(k * BLK, BLK), BLK)
        there = pl.ds(pl.multiple_of(t, BLK), BLK)
        return (
            pltpu.make_async_copy(a_hbm.at[e, there], a.at[here], sems.at[0, k]),
            pltpu.make_async_copy(g_hbm.at[e, there], g.at[here], sems.at[1, k]),
        )

    def begin(k, carry):
        for c in copies(k):
            c.start()
        return carry

    lax.fori_loop(0, nblk, begin, 0)

    def some(j, carry):
        for k in range(chunk):
            for c in copies(j * chunk + k):
                c.wait()
        at = pl.ds(pl.multiple_of(j * (chunk * BLK), BLK), chunk * BLK)
        for i, rows in enumerate((a, g)):
            x = jnp.dot(rows[at, :], w[i], preferred_element_type=F32)
            for k in range(chunk):
                b = j * chunk + k
                live = lax.broadcasted_iota(I32, (BLK, 128), 0) < locate(first + b, lens)[2]
                coded, code = encode(jnp.where(live, x[k * BLK : (k + 1) * BLK], 0.0))
                q[pl.ds(pl.multiple_of(b * BLK, BLK), BLK), i * 128 : (i + 1) * 128] = coded
                codes[b, :, i * 128 : (i + 1) * 128] = code
        return carry

    lax.fori_loop(0, nblk // chunk, some, 0)
    foot(q, nblk * BLK, codes, nblk)


def far_piece(lens, w, a, g, nblk, s):
    rows = nblk * BLK
    chunk = next(c for c in (4, 3, 2, 1) if nblk % c == 0)
    return pl.pallas_call(
        functools.partial(far_kernel, nblk, chunk, s),
        out_shape=jax.ShapeDtypeStruct((rows + FOOT, 256), I16),
        in_specs=[pl.BlockSpec(memory_space=SMEM), pl.BlockSpec(memory_space=VMEM)]
        + [pl.BlockSpec(memory_space=pl.ANY)] * 2,
        out_specs=pl.BlockSpec(memory_space=VMEM),
        scratch_shapes=[
            VMEM((rows, a.shape[2]), BF16),
            VMEM((rows, a.shape[2]), BF16),
            VMEM((FOOT, 1, 256), F32),
            pltpu.SemaphoreType.DMA((2, nblk)),
        ],
        compiler_params=pltpu.CompilerParams(vmem_limit_bytes=50 * MIB),
        cost_estimate=pl.CostEstimate(flops=1000, bytes_accessed=1000, transcendentals=0),
    )(lens, w, a, g)


def scales_of(refs, rows, count):
    return [scale_of(r[rows:, :].astype(I32).astype(F32)) * (1.0 / TOP) for r in refs]


def value(ref, start, n):
    return ref[pl.ds(start, n), :].astype(I32).astype(F32)


def middle_kernel(rows, sub, step, which, q0, q1, q2, q3, *rest):
    refs, outs, (scales, codes) = (q0, q1, q2, q3), rest[:-2], rest[-2:]
    two = position()[1]
    for i, s in enumerate(scales_of(refs, rows, rows // BLK)):
        scales[i] = s
    for s, out in zip(which, outs):
        begin = (two + s) % 4 * sub

        def some(j, carry, out=out, begin=begin):
            at = pl.multiple_of(begin + j * step, step)
            total = None
            for i, r in enumerate(refs):
                v = value(r, at, step) * scales[i, pl.ds(at // BLK, 1), :]
                total = v if total is None else total + v
            coded, code = encode(total)
            out[pl.ds(pl.multiple_of(j * step, step), step), :] = coded
            codes[j] = code
            return carry

        lax.fori_loop(0, sub // step, some, 0, unroll=2)
        foot(out, sub, codes, sub // step)


def middle_sum(pieces, rows, sub, step, which):
    return pl.pallas_call(
        functools.partial(middle_kernel, rows, sub, step, which),
        out_shape=[jax.ShapeDtypeStruct((sub + FOOT, 256), I16)] * len(which),
        in_specs=[pl.BlockSpec(memory_space=VMEM)] * 4,
        out_specs=[pl.BlockSpec(memory_space=VMEM)] * len(which),
        scratch_shapes=[VMEM((4, FOOT, 256), F32), VMEM((FOOT, 1, 256), F32)],
        compiler_params=pltpu.CompilerParams(vmem_limit_bytes=4 * MIB),
        cost_estimate=pl.CostEstimate(
            flops=rows * 64 * 8 * len(which), bytes_accessed=rows * 256 * 2, transcendentals=0
        ),
    )(*pieces)


def last_kernel(sub, step, r0, r1, r2, r3, out):
    refs = (r0, r1, r2, r3)
    scales = scales_of(refs, sub, sub // step)
    for j in range(sub // step):
        total = None
        for i, r in enumerate(refs):
            v = value(r, j * step, step) * scales[i][j : j + 1, :]
            total = v if total is None else total + v
        out[j * step : (j + 1) * step, :] = total.astype(BF16)


def last_sum(pieces, sub, step):
    return pl.pallas_call(
        functools.partial(last_kernel, sub, step),
        out_shape=jax.ShapeDtypeStruct((sub, 256), BF16),
        in_specs=[pl.BlockSpec(memory_space=VMEM)] * 4,
        out_specs=pl.BlockSpec(memory_space=VMEM),
        compiler_params=pltpu.CompilerParams(vmem_limit_bytes=3 * MIB),
        cost_estimate=pl.CostEstimate(
            flops=sub * 256 * 8, bytes_accessed=sub * 256 * 10, transcendentals=0
        ),
    )(*pieces)


def precondition(grad, first, second):
    top = 0.9 * first + 0.1 * grad
    return top / (jnp.sqrt(0.999 * second + 0.001 * grad * grad) + 1e-08)


def join_kernel(r0, r1, r2, r3, out):
    two = position()[1]
    for s, r in enumerate((r0, r1, r2, r3)):
        out[(two - s) % 4] = r[...]


def join(parts):
    sub = parts[0].shape[0]
    return pl.pallas_call(
        join_kernel,
        out_shape=jax.ShapeDtypeStruct((4, sub, 256), BF16),
        in_specs=[pl.BlockSpec(memory_space=VMEM)] * 4,
        out_specs=pl.BlockSpec(memory_space=VMEM),
        compiler_params=pltpu.CompilerParams(vmem_limit_bytes=2 * MIB),
    )(*parts).reshape(4 * sub, 256)


def gather_sums(which, nblk, lens, pieces, a, g, up, down):
    tn = (((0,), (0,)), ((), ()))
    one = position()[0]
    for s, piece in zip(which, pieces):
        low = (one - s) % 4 * nblk

        def example(e, begin, piece=piece, low=low):
            count = (lens[e] + (BLK - 1)) // BLK
            first = jnp.clip(begin - low, 0, nblk)
            some = jnp.clip(begin + count - low, 0, nblk) - first
            skip = jnp.maximum(low - begin, 0)

            def add(b, n):
                packed = pl.ds(pl.multiple_of((first + b) * BLK, BLK), n * BLK)
                rows = pl.ds(pl.multiple_of((skip + b) * BLK, BLK), n * BLK)
                up[e] += lax.dot_general(
                    piece[packed, :128], g[e, rows, :], tn, preferred_element_type=F32
                )
                down[e] += lax.dot_general(
                    piece[packed, 128:], a[e, rows, :], tn, preferred_element_type=F32
                )

            for n in (16, 8, 4, 2, 1):

                @pl.when((some // n) % 2 == 1)
                def _(n=n):
                    add(some // (2 * n) * (2 * n), n)

            return begin + count

        lax.fori_loop(0, 6, example, jnp.int32(0))


def two_parts(x):
    big = x.astype(BF16)
    return big, (x - big.astype(F32)).astype(BF16)


def final_kernel(which, nblk, lens, *refs):
    n = len(which)
    a, g = refs[n : n + 2]
    parts = refs[n + 2 : n + 10]
    urp, uwp, dwp, drp, out, up, down, moments, wide2 = refs[n + 10 :]
    nt = (((1,), (1,)), ((), ()))
    me = dp_place()
    rank = parts[0].shape[0] // 4
    for s, part in enumerate(parts):
        at = pl.ds(pl.multiple_of((me - s) % 8 * rank, rank), rank)
        for i in range(4):
            moments[i, at, :] = part[i * rank : (i + 1) * rank, :]
    up[...] = jnp.zeros_like(up)
    down[...] = jnp.zeros_like(down)
    gather_sums(which, nblk, lens, refs[:n], a, g, up, down)

    sides = []
    for i, (width, side) in enumerate(((uwp, urp), (dwp, drp))):
        big, rest = two_parts(width[...])
        wide2[i, :64, :] = big
        wide2[i, 64:, :] = rest
        sides.append(side[...])

    def examples(j, carry):
        for i, grad in enumerate((up, down)):
            pre = jnp.concatenate(
                [
                    precondition(grad[2 * j + k], moments[2 * i], moments[2 * i + 1])
                    for k in range(2)
                ],
                axis=0,
            )
            big, rest = two_parts(pre)
            both = lax.dot_general(big, wide2[i], nt, preferred_element_type=F32)
            wide = both[:, :64] + (
                both[:, 64:]
                + lax.dot_general(rest, wide2[i, :64, :], nt, preferred_element_type=F32)
            )
            for k in range(2):
                out[2 * j + k, i * 64 : (i + 1) * 64, :] = jnp.dot(
                    sides[i],
                    wide[k * 128 : (k + 1) * 128],
                    precision=lax.Precision.HIGHEST,
                    preferred_element_type=F32,
                )
        return carry

    lax.fori_loop(0, 3, examples, 0)


def final_grads(which, nblk, lens, pieces, a, g, moments, *projectors):
    return pl.pallas_call(
        functools.partial(final_kernel, which, nblk),
        out_shape=jax.ShapeDtypeStruct((6, 128, 64), F32),
        in_specs=[pl.BlockSpec(memory_space=SMEM)]
        + [pl.BlockSpec(memory_space=VMEM)] * (len(which) + 14),
        out_specs=pl.BlockSpec(memory_space=VMEM),
        scratch_shapes=[
            VMEM((6, 128, 512), F32),
            VMEM((6, 128, 512), F32),
            VMEM((4, 128, 512), F32),
            VMEM((2, 128, 512), BF16),
        ],
        compiler_params=pltpu.CompilerParams(vmem_limit_bytes=6 * MIB),
        cost_estimate=pl.CostEstimate(
            flops=4 * nblk * len(which) * BLK * 512 * 128,
            bytes_accessed=nblk * len(which) * BLK * 512,
            transcendentals=0,
        ),
    )(lens, *pieces, a, g, *moments, *projectors)


def shifts(first, s):
    pairs = []
    for core in range(2):
        for z in range(4):
            for y in range(4):
                along_y = (core == 0) == first
                to = (z, (y + s) % 4) if along_y else ((z + s) % 4, y)
                pairs.append((core * 16 + z * 4 + y, core * 16 + to[0] * 4 + to[1]))
    return pairs


def send(x, first, s):
    return x if s == 0 else lax.ppermute(x, ("core", "z", "y"), shifts(first, s))


def features(nb, lens, w, moments, a, g, projectors):
    rows, sub, step, per = nb * BLK // 4, nb * BLK // 16, 32, nb // 4
    got = [None] * 4
    coded = far_piece(lens, w, a, g, per, 2)
    got[2] = send(coded, True, 2)
    coded, a, g = lax.optimization_barrier((coded, a, g))
    a, g = load(a, g)
    for s in (1, 3):
        got[s] = send(partial_piece(lens, w, a, g, per, s), True, s)
    got[2], own_lens = lax.optimization_barrier((got[2], lens))
    got[0] = partial_piece(own_lens, w, a, g, per, 0)
    got[0], moments = lax.optimization_barrier((got[0], moments))
    ring = ring_of(moments)
    back = [None] * 4
    for which in ((2,), (1, 3, 0)):
        for s, mid in zip(which, middle_sum(got, rows, sub, step, which)):
            back[s] = send(mid, False, s)
    own = last_sum(back, sub, step)
    piece = join([send(own, False, s) for s in range(4)])
    pieces = {s: send(piece, True, s) for s in (0, 1, 3, 2)}
    which = (0, 1, 3, 2)
    return final_grads(which, per, lens, [pieces[s] for s in which], a, g, ring, *projectors)


def share(x, axes, n):
    return lax.all_to_all(jnp.broadcast_to(x[None], (n,) + x.shape), axes, 0, 0, tiled=True)


def length_rows(lengths, rank, width):
    rows = jnp.stack([lengths // 64, lengths % 64])
    return jnp.pad(rows, ((0, rank - 2), (0, width - lengths.shape[0]))).astype(BF16)


def blocks_needed(rows, n):
    pairs = jnp.stack([r[2, :2, :n] for r in rows]).astype(F32)
    lengths = (pairs[:, 0] * 64.0 + pairs[:, 1]).astype(I32)
    return jnp.max(jnp.sum((lengths + (BLK - 1)) // BLK, axis=1))


def body(a, g, lengths, sf, ef, sra, srv, era, erv, urp, uwp, dwp, drp):
    param = ("z", "y")
    mine = jnp.stack([sf.T, ef, length_rows(lengths, sf.shape[1], sf.shape[0])])
    rows = ring_of(mine)
    w = turn(rows)
    moments = jnp.concatenate([era, erv, sra.T, srv.T], axis=0)
    projectors = (urp.T, uwp.T, dwp.T, drp.T)
    most = a.shape[0] * a.shape[1] // BLK
    sizes = [72, 80, most]
    need = blocks_needed(rows, lengths.shape[0])
    which = sum((need > nb).astype(I32) for nb in sizes[:-1])
    part = lax.switch(
        which,
        [functools.partial(features, nb) for nb in sizes],
        lengths,
        w,
        moments,
        a,
        g,
        projectors,
    )
    owned = jnp.swapaxes(part.reshape(6, 16, 8, 64), 0, 1)
    raw = jnp.sum(lax.all_to_all(owned, param, 0, 0, tiled=True), axis=0)
    square = jnp.sum(raw * raw, axis=(1, 2))
    square = share(jnp.broadcast_to(square[:, None], (6, 128)), param, 16)
    scale = lax.rsqrt(jnp.sum(square, axis=0)[:, 0] / 8192.0 + 1e-06)
    return (raw * scale[:, None, None]).reshape(6, 512)


def solution(mesh):
    grid = Mesh(mesh.devices.reshape(4, 2, 4, 4), ("x", "core", "z", "y"))
    dp, param = ("x", "core"), ("z", "y")
    in_specs = (
        P(dp, None, param),
        P(dp, None, param),
        P(dp),
        P(param, dp),
        P(dp, param),
        P(param, dp),
        P(param, dp),
        P(dp, param),
        P(dp, param),
        P(),
        P(param, None),
        P(param, None),
        P(),
    )
    return jax.shard_map(body, mesh=grid, in_specs=in_specs, out_specs=P(dp, param), check_vma=False)
```

```python
import functools

import jax
import jax.numpy as jnp
from jax import lax
from jax.experimental import pallas as pl
from jax.experimental.pallas import tpu as pltpu
from jax.sharding import Mesh, PartitionSpec as P

BLK = 128
FOOT = 32
RES = 128.0
TOP = 32767.0
MIB = 1024 * 1024
VMEM = pltpu.VMEM
SMEM = pltpu.SMEM
F32 = jnp.float32
BF16 = jnp.bfloat16
I16 = jnp.int16
I32 = jnp.int32


def divisor(n):
    return next(c for c in (4, 3, 2, 1) if n % c == 0)


def scale_code(peak):
    return jnp.ceil(jnp.log(jnp.maximum(peak, 1e-30)) * (RES / 0.6931471805599453)) + 1.0


def scale_of(code):
    return jnp.exp2(code * (1.0 / RES))


def encode(x):
    code = scale_code(jnp.max(jnp.abs(x), axis=0, keepdims=True))
    q = jnp.round(x * (TOP / scale_of(code)))
    return q.astype(I32).astype(I16), code


def position():
    y, z = lax.axis_index("y").astype(I32), lax.axis_index("z").astype(I32)
    zero = lax.axis_index("core") == 0
    return jnp.where(zero, y, z), jnp.where(zero, z, y)


def block_counts(lens):
    return [(lens[e] + (BLK - 1)) // BLK for e in range(lens.shape[0])]


def locate(b, lens):
    n = lens.shape[0]
    start, e, end = jnp.int32(0), jnp.int32(0), jnp.int32(0)
    for count in block_counts(lens):
        end = end + count
        past = b >= end
        start = jnp.where(past, end, start)
        e = jnp.where(past, e + 1, e)
    inside = e < n
    e = jnp.minimum(e, n - 1)
    t = jnp.where(inside, (b - start) * BLK, 0)
    return e, t, jnp.where(inside, jnp.clip(lens[e] - t, 0, BLK), 0)


def dp_place():
    return lax.axis_index("x").astype(I32) * 2 + lax.axis_index("core").astype(I32)


def ring_of(x):
    n = 8
    others = [
        lax.ppermute(x, ("x", "core"), [(i, (i + s) % n) for i in range(n)]) for s in range(1, n)
    ]
    return [x] + others


def load_kernel(a_hbm, g_hbm, a, g, sems):
    copies = [
        pltpu.make_async_copy(a_hbm, a, sems.at[0]),
        pltpu.make_async_copy(g_hbm, g, sems.at[1]),
    ]
    for c in copies:
        c.start()
    for c in copies:
        c.wait()


def load(a, g):
    return pl.pallas_call(
        load_kernel,
        out_shape=[VMEM(a.shape, a.dtype), VMEM(g.shape, g.dtype)],
        in_specs=[pl.BlockSpec(memory_space=pl.ANY)] * 2,
        out_specs=[pl.BlockSpec(memory_space=VMEM)] * 2,
        scratch_shapes=[pltpu.SemaphoreType.DMA((2,))],
        compiler_params=pltpu.CompilerParams(vmem_limit_bytes=24 * MIB),
        cost_estimate=pl.CostEstimate(flops=0, bytes_accessed=a.size * 4, transcendentals=0),
    )(a, g)


def turn_kernel(*refs):
    parts, (w, flat) = refs[:8], refs[8:]
    me = dp_place()
    rank = parts[0].shape[1]
    for s, part in enumerate(parts):
        at = pl.ds(pl.multiple_of((me - s) % 8 * rank, rank), rank)
        for i in range(2):
            flat[i, at, :] = part[i]
    for i in range(2):
        w[i] = flat[i].T


def turn(parts):
    _, rank, width = parts[0].shape
    return pl.pallas_call(
        turn_kernel,
        out_shape=jax.ShapeDtypeStruct((2, width, 8 * rank), BF16),
        in_specs=[pl.BlockSpec(memory_space=VMEM)] * 8,
        out_specs=pl.BlockSpec(memory_space=VMEM),
        scratch_shapes=[VMEM((2, 8 * rank, width), BF16)],
        compiler_params=pltpu.CompilerParams(vmem_limit_bytes=2 * MIB),
    )(*parts)


def foot(ref, start, codes, count):
    rows = [codes[k] for k in range(count)]
    rows.append(jnp.zeros((FOOT - count, 256), F32))
    ref[start:, :] = jnp.concatenate(rows, axis=0).astype(I32).astype(I16)


def partial_kernel(nblk, s, lens, w, a, g, q, codes):
    first = (position()[0] + s) % 4 * nblk

    def block(k, carry):
        e, t, count = locate(first + k, lens)
        t = pl.multiple_of(t, BLK)
        at = pl.ds(pl.multiple_of(k * BLK, BLK), BLK)
        live = lax.broadcasted_iota(I32, (BLK, 128), 0) < count
        for i, rows in enumerate((a, g)):
            x = jnp.dot(rows[e, pl.ds(t, BLK), :], w[i], preferred_element_type=F32)
            x = jnp.where(live, x, 0.0)
            coded, code = encode(x)
            q[at, i * 128 : (i + 1) * 128] = coded
            codes[k, :, i * 128 : (i + 1) * 128] = code
        return carry

    lax.fori_loop(0, nblk, block, 0, unroll=divisor(nblk))
    foot(q, nblk * BLK, codes, nblk)


def partial_piece(lens, w, a, g, nblk, s):
    rows = nblk * BLK
    return pl.pallas_call(
        functools.partial(partial_kernel, nblk, s),
        out_shape=jax.ShapeDtypeStruct((rows + FOOT, 256), I16),
        in_specs=[pl.BlockSpec(memory_space=SMEM)] + [pl.BlockSpec(memory_space=VMEM)] * 3,
        out_specs=pl.BlockSpec(memory_space=VMEM),
        scratch_shapes=[VMEM((FOOT, 1, 256), F32)],
        compiler_params=pltpu.CompilerParams(vmem_limit_bytes=2 * MIB),
        cost_estimate=pl.CostEstimate(
            flops=1000, bytes_accessed=1000, transcendentals=0
        ),
    )(lens, w, a, g)


def far_kernel(nblk, chunk, s, lens, w, a_hbm, g_hbm, q, a, g, codes, sems):
    first = (position()[0] + s) % 4 * nblk

    def copies(k):
        e, t, _ = locate(first + k, lens)
        here = pl.ds(pl.multiple_of(k * BLK, BLK), BLK)
        there = pl.ds(pl.multiple_of(t, BLK), BLK)
        return (
            pltpu.make_async_copy(a_hbm.at[e, there], a.at[here], sems.at[0, k]),
            pltpu.make_async_copy(g_hbm.at[e, there], g.at[here], sems.at[1, k]),
        )

    def begin(k, carry):
        for c in copies(k):
            c.start()
        return carry

    lax.fori_loop(0, nblk, begin, 0)

    def some(j, carry):
        for k in range(chunk):
            for c in copies(j * chunk + k):
                c.wait()
        at = pl.ds(pl.multiple_of(j * (chunk * BLK), BLK), chunk * BLK)
        for i, rows in enumerate((a, g)):
            x = jnp.dot(rows[at, :], w[i], preferred_element_type=F32)
            for k in range(chunk):
                b = j * chunk + k
                live = lax.broadcasted_iota(I32, (BLK, 128), 0) < locate(first + b, lens)[2]
                coded, code = encode(jnp.where(live, x[k * BLK : (k + 1) * BLK], 0.0))
                q[pl.ds(pl.multiple_of(b * BLK, BLK), BLK), i * 128 : (i + 1) * 128] = coded
                codes[b, :, i * 128 : (i + 1) * 128] = code
        return carry

    lax.fori_loop(0, nblk // chunk, some, 0)
    foot(q, nblk * BLK, codes, nblk)


def far_piece(lens, w, a, g, nblk, s):
    rows = nblk * BLK
    chunk = 2 if nblk % 2 == 0 else 1
    return pl.pallas_call(
        functools.partial(far_kernel, nblk, chunk, s),
        out_shape=jax.ShapeDtypeStruct((rows + FOOT, 256), I16),
        in_specs=[pl.BlockSpec(memory_space=SMEM), pl.BlockSpec(memory_space=VMEM)]
        + [pl.BlockSpec(memory_space=pl.ANY)] * 2,
        out_specs=pl.BlockSpec(memory_space=VMEM),
        scratch_shapes=[
            VMEM((rows, a.shape[2]), BF16),
            VMEM((rows, a.shape[2]), BF16),
            VMEM((FOOT, 1, 256), F32),
            pltpu.SemaphoreType.DMA((2, nblk)),
        ],
        compiler_params=pltpu.CompilerParams(vmem_limit_bytes=50 * MIB),
        cost_estimate=pl.CostEstimate(flops=1000, bytes_accessed=1000, transcendentals=0),
    )(lens, w, a, g)


def scales_of(refs, rows, count):
    return [scale_of(r[rows:, :].astype(I32).astype(F32)) * (1.0 / TOP) for r in refs]


def value(ref, start, n):
    return ref[pl.ds(start, n), :].astype(I32).astype(F32)


def middle_kernel(rows, sub, step, which, q0, q1, q2, q3, *rest):
    refs, outs, (scales, codes) = (q0, q1, q2, q3), rest[:-2], rest[-2:]
    two = position()[1]
    for i, s in enumerate(scales_of(refs, rows, rows // BLK)):
        scales[i] = s
    for s, out in zip(which, outs):
        begin = (two + s) % 4 * sub

        def some(j, carry, out=out, begin=begin):
            at = pl.multiple_of(begin + j * step, step)
            total = None
            for i, r in enumerate(refs):
                v = value(r, at, step) * scales[i, pl.ds(at // BLK, 1), :]
                total = v if total is None else total + v
            coded, code = encode(total)
            out[pl.ds(pl.multiple_of(j * step, step), step), :] = coded
            codes[j] = code
            return carry

        lax.fori_loop(0, sub // step, some, 0, unroll=divisor(sub // step))
        foot(out, sub, codes, sub // step)


def middle_sum(pieces, rows, sub, step, which):
    return pl.pallas_call(
        functools.partial(middle_kernel, rows, sub, step, which),
        out_shape=[jax.ShapeDtypeStruct((sub + FOOT, 256), I16)] * len(which),
        in_specs=[pl.BlockSpec(memory_space=VMEM)] * 4,
        out_specs=[pl.BlockSpec(memory_space=VMEM)] * len(which),
        scratch_shapes=[VMEM((4, FOOT, 256), F32), VMEM((FOOT, 1, 256), F32)],
        compiler_params=pltpu.CompilerParams(vmem_limit_bytes=4 * MIB),
        cost_estimate=pl.CostEstimate(
            flops=rows * 64 * 8 * len(which), bytes_accessed=rows * 256 * 2, transcendentals=0
        ),
    )(*pieces)


def last_kernel(sub, step, r0, r1, r2, r3, out):
    refs = (r0, r1, r2, r3)
    scales = scales_of(refs, sub, sub // step)
    for j in range(sub // step):
        total = None
        for i, r in enumerate(refs):
            v = value(r, j * step, step) * scales[i][j : j + 1, :]
            total = v if total is None else total + v
        out[j * step : (j + 1) * step, :] = total.astype(BF16)


def last_sum(pieces, sub, step):
    return pl.pallas_call(
        functools.partial(last_kernel, sub, step),
        out_shape=jax.ShapeDtypeStruct((sub, 256), BF16),
        in_specs=[pl.BlockSpec(memory_space=VMEM)] * 4,
        out_specs=pl.BlockSpec(memory_space=VMEM),
        compiler_params=pltpu.CompilerParams(vmem_limit_bytes=3 * MIB),
        cost_estimate=pl.CostEstimate(
            flops=sub * 256 * 8, bytes_accessed=sub * 256 * 10, transcendentals=0
        ),
    )(*pieces)


def precondition(grad, first, second):
    return (first + 0.1 * grad) / (jnp.sqrt(second + 0.001 * grad * grad) + 1e-08)


def join_kernel(r0, r1, r2, r3, out):
    two = position()[1]
    for s, r in enumerate((r0, r1, r2, r3)):
        out[(two - s) % 4] = r[...]


def join(parts):
    sub = parts[0].shape[0]
    return pl.pallas_call(
        join_kernel,
        out_shape=jax.ShapeDtypeStruct((4, sub, 256), BF16),
        in_specs=[pl.BlockSpec(memory_space=VMEM)] * 4,
        out_specs=pl.BlockSpec(memory_space=VMEM),
        compiler_params=pltpu.CompilerParams(vmem_limit_bytes=2 * MIB),
    )(*parts).reshape(4 * sub, 256)


def gather_sums(which, nblk, lens, pieces, a, g, up, down):
    tn = (((0,), (0,)), ((), ()))
    one = position()[0]
    for s, piece in zip(which, pieces):
        low = (one - s) % 4 * nblk

        def example(e, begin, piece=piece, low=low):
            count = (lens[e] + (BLK - 1)) // BLK
            first = jnp.clip(begin - low, 0, nblk)
            some = jnp.clip(begin + count - low, 0, nblk) - first
            skip = jnp.maximum(low - begin, 0)

            def add(b, n):
                packed = pl.ds(pl.multiple_of((first + b) * BLK, BLK), n * BLK)
                rows = pl.ds(pl.multiple_of((skip + b) * BLK, BLK), n * BLK)
                up[e] += lax.dot_general(
                    piece[packed, :128], g[e, rows, :], tn, preferred_element_type=F32
                )
                down[e] += lax.dot_general(
                    piece[packed, 128:], a[e, rows, :], tn, preferred_element_type=F32
                )

            def eight(i, carry):
                add(i * 8, 8)
                return carry

            lax.fori_loop(0, some // 8, eight, 0)
            for n in (4, 2, 1):

                @pl.when((some // n) % 2 == 1)
                def _(n=n):
                    add(some // (2 * n) * (2 * n), n)

            return begin + count

        lax.fori_loop(0, 6, example, jnp.int32(0))


def two_parts(x):
    big = x.astype(BF16)
    return big, (x - big.astype(F32)).astype(BF16)


def final_kernel(which, nblk, lens, *refs):
    n = len(which)
    a, g = refs[n : n + 2]
    parts = refs[n + 2 : n + 10]
    urp, uwp, dwp, drp, out, up, down, moments, wide2 = refs[n + 10 :]
    nt = (((1,), (1,)), ((), ()))
    me = dp_place()
    rank = parts[0].shape[0] // 4
    for s, part in enumerate(parts):
        at = pl.ds(pl.multiple_of((me - s) % 8 * rank, rank), rank)
        for i in range(4):
            moments[i, at, :] = part[i * rank : (i + 1) * rank, :] * (0.9, 0.999)[i % 2]
    up[...] = jnp.zeros_like(up)
    down[...] = jnp.zeros_like(down)
    gather_sums(which, nblk, lens, refs[:n], a, g, up, down)

    sides = []
    for i, (width, side) in enumerate(((uwp, urp), (dwp, drp))):
        big, rest = two_parts(width[...])
        wide2[i, :64, :] = big
        wide2[i, 64:, :] = rest
        sides.append(side[...])

    def examples(j, carry):
        for i, grad in enumerate((up, down)):
            pre = jnp.concatenate(
                [
                    precondition(grad[2 * j + k], moments[2 * i], moments[2 * i + 1])
                    for k in range(2)
                ],
                axis=0,
            )
            big, rest = two_parts(pre)
            both = lax.dot_general(big, wide2[i], nt, preferred_element_type=F32)
            wide = both[:, :64] + (
                both[:, 64:]
                + lax.dot_general(rest, wide2[i, :64, :], nt, preferred_element_type=F32)
            )
            for k in range(2):
                out[2 * j + k, i * 64 : (i + 1) * 64, :] = jnp.dot(
                    sides[i],
                    wide[k * 128 : (k + 1) * 128],
                    precision=lax.Precision.HIGHEST,
                    preferred_element_type=F32,
                )
        return carry

    lax.fori_loop(0, 3, examples, 0)


def final_grads(which, nblk, lens, pieces, a, g, moments, *projectors):
    return pl.pallas_call(
        functools.partial(final_kernel, which, nblk),
        out_shape=jax.ShapeDtypeStruct((6, 128, 64), F32),
        in_specs=[pl.BlockSpec(memory_space=SMEM)]
        + [pl.BlockSpec(memory_space=VMEM)] * (len(which) + 14),
        out_specs=pl.BlockSpec(memory_space=VMEM),
        scratch_shapes=[
            VMEM((6, 128, 512), F32),
            VMEM((6, 128, 512), F32),
            VMEM((4, 128, 512), F32),
            VMEM((2, 128, 512), BF16),
        ],
        compiler_params=pltpu.CompilerParams(vmem_limit_bytes=6 * MIB),
        cost_estimate=pl.CostEstimate(
            flops=4 * nblk * len(which) * BLK * 512 * 128,
            bytes_accessed=nblk * len(which) * BLK * 512,
            transcendentals=0,
        ),
    )(lens, *pieces, a, g, *moments, *projectors)


def shifts(first, s):
    pairs = []
    for core in range(2):
        for z in range(4):
            for y in range(4):
                along_y = (core == 0) == first
                to = (z, (y + s) % 4) if along_y else ((z + s) % 4, y)
                pairs.append((core * 16 + z * 4 + y, core * 16 + to[0] * 4 + to[1]))
    return pairs


def send(x, first, s):
    return x if s == 0 else lax.ppermute(x, ("core", "z", "y"), shifts(first, s))


def features(nb, lens, w, moments, a, g, projectors):
    rows, sub, step, per = nb * BLK // 4, nb * BLK // 16, 32, nb // 4
    got = [None] * 4
    coded = far_piece(lens, w, a, g, per, 2)
    got[2] = send(coded, True, 2)
    coded, a, g = lax.optimization_barrier((coded, a, g))
    a, g = load(a, g)
    for s in (1, 3):
        got[s] = send(partial_piece(lens, w, a, g, per, s), True, s)
    got[2], own_lens = lax.optimization_barrier((got[2], lens))
    got[0] = partial_piece(own_lens, w, a, g, per, 0)
    got[0], moments = lax.optimization_barrier((got[0], moments))
    ring = ring_of(moments)
    back = [None] * 4
    for which in ((2,), (1, 3, 0)):
        for s, mid in zip(which, middle_sum(got, rows, sub, step, which)):
            back[s] = send(mid, False, s)
    own = last_sum(back, sub, step)
    piece = join([send(own, False, s) for s in range(4)])
    pieces = {s: send(piece, True, s) for s in (0, 1, 3, 2)}
    which = (0, 1, 3, 2)
    return final_grads(which, per, lens, [pieces[s] for s in which], a, g, ring, *projectors)


def share(x, axes, n):
    return lax.all_to_all(jnp.broadcast_to(x[None], (n,) + x.shape), axes, 0, 0, tiled=True)


def length_rows(lengths, rank, width):
    rows = jnp.stack([lengths // 64, lengths % 64])
    return jnp.pad(rows, ((0, rank - 2), (0, width - lengths.shape[0]))).astype(BF16)


def blocks_needed(rows, n):
    pairs = jnp.stack([r[2, :2, :n] for r in rows]).astype(F32)
    lengths = (pairs[:, 0] * 64.0 + pairs[:, 1]).astype(I32)
    return jnp.max(jnp.sum((lengths + (BLK - 1)) // BLK, axis=1))


def body(a, g, lengths, sf, ef, sra, srv, era, erv, urp, uwp, dwp, drp):
    param = ("z", "y")
    mine = jnp.stack([sf.T, ef, length_rows(lengths, sf.shape[1], sf.shape[0])])
    rows = ring_of(mine)
    w = turn(rows)
    moments = jnp.concatenate([era, erv, sra.T, srv.T], axis=0)
    projectors = (urp.T, uwp.T, dwp.T, drp.T)
    most = a.shape[0] * a.shape[1] // BLK
    sizes = [80, most]
    need = blocks_needed(rows, lengths.shape[0])
    which = sum((need > nb).astype(I32) for nb in sizes[:-1])
    part = lax.switch(
        which,
        [functools.partial(features, nb) for nb in sizes],
        lengths,
        w,
        moments,
        a,
        g,
        projectors,
    )
    owned = jnp.swapaxes(part.reshape(6, 16, 8, 64), 0, 1)
    raw = jnp.sum(lax.all_to_all(owned, param, 0, 0, tiled=True), axis=0)
    square = jnp.sum(raw * raw, axis=(1, 2))
    square = share(jnp.broadcast_to(square[:, None], (6, 128)), param, 16)
    scale = lax.rsqrt(jnp.sum(square, axis=0)[:, 0] / 8192.0 + 1e-06)
    return (raw * scale[:, None, None]).reshape(6, 512)


def solution(mesh):
    grid = Mesh(mesh.devices.reshape(4, 2, 4, 4), ("x", "core", "z", "y"))
    dp, param = ("x", "core"), ("z", "y")
    in_specs = (
        P(dp, None, param),
        P(dp, None, param),
        P(dp),
        P(param, dp),
        P(dp, param),
        P(param, dp),
        P(param, dp),
        P(dp, param),
        P(dp, param),
        P(),
        P(param, None),
        P(param, None),
        P(),
    )
    return jax.shard_map(body, mesh=grid, in_specs=in_specs, out_specs=P(dp, param), check_vma=False)
```

```python
import functools

import jax
import jax.numpy as jnp
from jax import lax
from jax.experimental import pallas as pl
from jax.experimental.pallas import tpu as pltpu
from jax.sharding import Mesh, PartitionSpec as P

BLK = 128
FOOT = 32
RES = 128.0
TOP = 32767.0
MIB = 1024 * 1024
VMEM = pltpu.VMEM
SMEM = pltpu.SMEM
F32 = jnp.float32
BF16 = jnp.bfloat16
I16 = jnp.int16
I32 = jnp.int32


def divisor(n):
    return next(c for c in (4, 3, 2, 1) if n % c == 0)


def scale_code(peak):
    return jnp.ceil(jnp.log(jnp.maximum(peak, 1e-30)) * (RES / 0.6931471805599453)) + 1.0


def scale_of(code):
    return jnp.exp2(code * (1.0 / RES))


def encode(x):
    code = scale_code(jnp.max(jnp.abs(x), axis=0, keepdims=True))
    q = jnp.round(x * (TOP / scale_of(code)))
    return q.astype(I32).astype(I16), code


def position():
    y, z = lax.axis_index("y").astype(I32), lax.axis_index("z").astype(I32)
    zero = lax.axis_index("core") == 0
    return jnp.where(zero, y, z), jnp.where(zero, z, y)


def block_counts(lens):
    return [(lens[e] + (BLK - 1)) // BLK for e in range(lens.shape[0])]


def locate(b, lens):
    n = lens.shape[0]
    start, e, end = jnp.int32(0), jnp.int32(0), jnp.int32(0)
    for count in block_counts(lens):
        end = end + count
        past = b >= end
        start = jnp.where(past, end, start)
        e = jnp.where(past, e + 1, e)
    inside = e < n
    e = jnp.minimum(e, n - 1)
    t = jnp.where(inside, (b - start) * BLK, 0)
    return e, t, jnp.where(inside, jnp.clip(lens[e] - t, 0, BLK), 0)


def dp_place():
    return lax.axis_index("x").astype(I32) * 2 + lax.axis_index("core").astype(I32)


def ring_of(x):
    n = 8
    others = [
        lax.ppermute(x, ("x", "core"), [(i, (i + s) % n) for i in range(n)]) for s in range(1, n)
    ]
    return [x] + others


def load_kernel(a_hbm, g_hbm, a, g, sems):
    copies = [
        pltpu.make_async_copy(a_hbm, a, sems.at[0]),
        pltpu.make_async_copy(g_hbm, g, sems.at[1]),
    ]
    for c in copies:
        c.start()
    for c in copies:
        c.wait()


def load(a, g):
    return pl.pallas_call(
        load_kernel,
        out_shape=[VMEM(a.shape, a.dtype), VMEM(g.shape, g.dtype)],
        in_specs=[pl.BlockSpec(memory_space=pl.ANY)] * 2,
        out_specs=[pl.BlockSpec(memory_space=VMEM)] * 2,
        scratch_shapes=[pltpu.SemaphoreType.DMA((2,))],
        compiler_params=pltpu.CompilerParams(vmem_limit_bytes=24 * MIB),
        cost_estimate=pl.CostEstimate(flops=0, bytes_accessed=a.size * 4, transcendentals=0),
    )(a, g)


def turn_kernel(*refs):
    parts, (w, flat) = refs[:8], refs[8:]
    me = dp_place()
    rank = parts[0].shape[1]
    for s, part in enumerate(parts):
        at = pl.ds(pl.multiple_of((me - s) % 8 * rank, rank), rank)
        for i in range(2):
            flat[i, at, :] = part[i]
    for i in range(2):
        w[i] = flat[i].T


def turn(parts):
    _, rank, width = parts[0].shape
    return pl.pallas_call(
        turn_kernel,
        out_shape=jax.ShapeDtypeStruct((2, width, 8 * rank), BF16),
        in_specs=[pl.BlockSpec(memory_space=VMEM)] * 8,
        out_specs=pl.BlockSpec(memory_space=VMEM),
        scratch_shapes=[VMEM((2, 8 * rank, width), BF16)],
        compiler_params=pltpu.CompilerParams(vmem_limit_bytes=2 * MIB),
    )(*parts)


def foot(ref, start, codes, count):
    rows = [codes[k] for k in range(count)]
    rows.append(jnp.zeros((FOOT - count, 256), F32))
    ref[start:, :] = jnp.concatenate(rows, axis=0).astype(I32).astype(I16)


def partial_kernel(nblk, s, lens, w, a, g, q, codes):
    first = (position()[0] + s) % 4 * nblk

    def block(k, carry):
        e, t, count = locate(first + k, lens)
        t = pl.multiple_of(t, BLK)
        at = pl.ds(pl.multiple_of(k * BLK, BLK), BLK)
        live = lax.broadcasted_iota(I32, (BLK, 128), 0) < count
        for i, rows in enumerate((a, g)):
            x = jnp.dot(rows[e, pl.ds(t, BLK), :], w[i], preferred_element_type=F32)
            x = jnp.where(live, x, 0.0)
            coded, code = encode(x)
            q[at, i * 128 : (i + 1) * 128] = coded
            codes[k, :, i * 128 : (i + 1) * 128] = code
        return carry

    lax.fori_loop(0, nblk, block, 0, unroll=divisor(nblk))
    foot(q, nblk * BLK, codes, nblk)


def partial_piece(lens, w, a, g, nblk, s):
    rows = nblk * BLK
    return pl.pallas_call(
        functools.partial(partial_kernel, nblk, s),
        out_shape=jax.ShapeDtypeStruct((rows + FOOT, 256), I16),
        in_specs=[pl.BlockSpec(memory_space=SMEM)] + [pl.BlockSpec(memory_space=VMEM)] * 3,
        out_specs=pl.BlockSpec(memory_space=VMEM),
        scratch_shapes=[VMEM((FOOT, 1, 256), F32)],
        compiler_params=pltpu.CompilerParams(vmem_limit_bytes=2 * MIB),
        cost_estimate=pl.CostEstimate(
            flops=1000, bytes_accessed=1000, transcendentals=0
        ),
    )(lens, w, a, g)


def far_kernel(nblk, chunk, s, lens, w, a_hbm, g_hbm, q, a, g, codes, sems):
    first = (position()[0] + s) % 4 * nblk

    def copies(k):
        e, t, _ = locate(first + k, lens)
        here = pl.ds(pl.multiple_of(k * BLK, BLK), BLK)
        there = pl.ds(pl.multiple_of(t, BLK), BLK)
        return (
            pltpu.make_async_copy(a_hbm.at[e, there], a.at[here], sems.at[0, k]),
            pltpu.make_async_copy(g_hbm.at[e, there], g.at[here], sems.at[1, k]),
        )

    def begin(k, carry):
        for c in copies(k):
            c.start()
        return carry

    lax.fori_loop(0, nblk, begin, 0)

    def some(j, carry):
        for k in range(chunk):
            for c in copies(j * chunk + k):
                c.wait()
        at = pl.ds(pl.multiple_of(j * (chunk * BLK), BLK), chunk * BLK)
        for i, rows in enumerate((a, g)):
            x = jnp.dot(rows[at, :], w[i], preferred_element_type=F32)
            for k in range(chunk):
                b = j * chunk + k
                live = lax.broadcasted_iota(I32, (BLK, 128), 0) < locate(first + b, lens)[2]
                coded, code = encode(jnp.where(live, x[k * BLK : (k + 1) * BLK], 0.0))
                q[pl.ds(pl.multiple_of(b * BLK, BLK), BLK), i * 128 : (i + 1) * 128] = coded
                codes[b, :, i * 128 : (i + 1) * 128] = code
        return carry

    lax.fori_loop(0, nblk // chunk, some, 0)
    foot(q, nblk * BLK, codes, nblk)


def far_piece(lens, w, a, g, nblk, s):
    rows = nblk * BLK
    chunk = 2 if nblk % 2 == 0 else 1
    return pl.pallas_call(
        functools.partial(far_kernel, nblk, chunk, s),
        out_shape=jax.ShapeDtypeStruct((rows + FOOT, 256), I16),
        in_specs=[pl.BlockSpec(memory_space=SMEM), pl.BlockSpec(memory_space=VMEM)]
        + [pl.BlockSpec(memory_space=pl.ANY)] * 2,
        out_specs=pl.BlockSpec(memory_space=VMEM),
        scratch_shapes=[
            VMEM((rows, a.shape[2]), BF16),
            VMEM((rows, a.shape[2]), BF16),
            VMEM((FOOT, 1, 256), F32),
            pltpu.SemaphoreType.DMA((2, nblk)),
        ],
        compiler_params=pltpu.CompilerParams(vmem_limit_bytes=50 * MIB),
        cost_estimate=pl.CostEstimate(flops=1000, bytes_accessed=1000, transcendentals=0),
    )(lens, w, a, g)


def scales_of(refs, rows, count):
    return [scale_of(r[rows:, :].astype(I32).astype(F32)) * (1.0 / TOP) for r in refs]


def value(ref, start, n):
    return ref[pl.ds(start, n), :].astype(I32).astype(F32)


def middle_kernel(rows, sub, step, which, q0, q1, q2, q3, *rest):
    refs, outs, (scales, codes) = (q0, q1, q2, q3), rest[:-2], rest[-2:]
    two = position()[1]
    for i, s in enumerate(scales_of(refs, rows, rows // BLK)):
        scales[i] = s
    for s, out in zip(which, outs):
        begin = (two + s) % 4 * sub

        def some(j, carry, out=out, begin=begin):
            at = pl.multiple_of(begin + j * step, step)
            total = None
            for i, r in enumerate(refs):
                v = value(r, at, step) * scales[i, pl.ds(at // BLK, 1), :]
                total = v if total is None else total + v
            coded, code = encode(total)
            out[pl.ds(pl.multiple_of(j * step, step), step), :] = coded
            codes[j] = code
            return carry

        lax.fori_loop(0, sub // step, some, 0, unroll=divisor(sub // step))
        foot(out, sub, codes, sub // step)


def middle_sum(pieces, rows, sub, step, which):
    return pl.pallas_call(
        functools.partial(middle_kernel, rows, sub, step, which),
        out_shape=[jax.ShapeDtypeStruct((sub + FOOT, 256), I16)] * len(which),
        in_specs=[pl.BlockSpec(memory_space=VMEM)] * 4,
        out_specs=[pl.BlockSpec(memory_space=VMEM)] * len(which),
        scratch_shapes=[VMEM((4, FOOT, 256), F32), VMEM((FOOT, 1, 256), F32)],
        compiler_params=pltpu.CompilerParams(vmem_limit_bytes=4 * MIB),
        cost_estimate=pl.CostEstimate(
            flops=rows * 64 * 8 * len(which), bytes_accessed=rows * 256 * 2, transcendentals=0
        ),
    )(*pieces)


def last_kernel(sub, step, r0, r1, r2, r3, out):
    refs = (r0, r1, r2, r3)
    scales = scales_of(refs, sub, sub // step)
    for j in range(sub // step):
        total = None
        for i, r in enumerate(refs):
            v = value(r, j * step, step) * scales[i][j : j + 1, :]
            total = v if total is None else total + v
        out[j * step : (j + 1) * step, :] = total.astype(BF16)


def last_sum(pieces, sub, step):
    return pl.pallas_call(
        functools.partial(last_kernel, sub, step),
        out_shape=jax.ShapeDtypeStruct((sub, 256), BF16),
        in_specs=[pl.BlockSpec(memory_space=VMEM)] * 4,
        out_specs=pl.BlockSpec(memory_space=VMEM),
        compiler_params=pltpu.CompilerParams(vmem_limit_bytes=3 * MIB),
        cost_estimate=pl.CostEstimate(
            flops=sub * 256 * 8, bytes_accessed=sub * 256 * 10, transcendentals=0
        ),
    )(*pieces)


def precondition(grad, first, second):
    return (first + 0.1 * grad) / (jnp.sqrt(second + 0.001 * grad * grad) + 1e-08)


def join_kernel(r0, r1, r2, r3, out):
    two = position()[1]
    for s, r in enumerate((r0, r1, r2, r3)):
        out[(two - s) % 4] = r[...]


def join(parts):
    sub = parts[0].shape[0]
    return pl.pallas_call(
        join_kernel,
        out_shape=jax.ShapeDtypeStruct((4, sub, 256), BF16),
        in_specs=[pl.BlockSpec(memory_space=VMEM)] * 4,
        out_specs=pl.BlockSpec(memory_space=VMEM),
        compiler_params=pltpu.CompilerParams(vmem_limit_bytes=2 * MIB),
    )(*parts).reshape(4 * sub, 256)


def gather_sums(which, nblk, lens, pieces, a, g, up, down):
    tn = (((0,), (0,)), ((), ()))
    one = position()[0]
    for s, piece in zip(which, pieces):
        low = (one - s) % 4 * nblk

        def example(e, begin, piece=piece, low=low):
            count = (lens[e] + (BLK - 1)) // BLK
            first = jnp.clip(begin - low, 0, nblk)
            some = jnp.clip(begin + count - low, 0, nblk) - first
            skip = jnp.maximum(low - begin, 0)

            def add(b, n):
                packed = pl.ds(pl.multiple_of((first + b) * BLK, BLK), n * BLK)
                rows = pl.ds(pl.multiple_of((skip + b) * BLK, BLK), n * BLK)
                up[e] += lax.dot_general(
                    piece[packed, :128], g[e, rows, :], tn, preferred_element_type=F32
                )
                down[e] += lax.dot_general(
                    piece[packed, 128:], a[e, rows, :], tn, preferred_element_type=F32
                )

            def eight(i, carry):
                add(i * 8, 8)
                return carry

            lax.fori_loop(0, some // 8, eight, 0)
            for n in (4, 2, 1):

                @pl.when((some // n) % 2 == 1)
                def _(n=n):
                    add(some // (2 * n) * (2 * n), n)

            return begin + count

        lax.fori_loop(0, 6, example, jnp.int32(0))


def two_parts(x):
    big = x.astype(BF16)
    return big, (x - big.astype(F32)).astype(BF16)


def final_kernel(which, nblk, lens, *refs):
    n = len(which)
    a, g = refs[n : n + 2]
    parts = refs[n + 2 : n + 10]
    urp, uwp, dwp, drp, out, up, down, moments, wide2 = refs[n + 10 :]
    nt = (((1,), (1,)), ((), ()))
    me = dp_place()
    rank = parts[0].shape[0] // 4
    for s, part in enumerate(parts):
        at = pl.ds(pl.multiple_of((me - s) % 8 * rank, rank), rank)
        for i in range(4):
            moments[i, at, :] = part[i * rank : (i + 1) * rank, :] * (0.9, 0.999)[i % 2]
    up[...] = jnp.zeros_like(up)
    down[...] = jnp.zeros_like(down)
    gather_sums(which, nblk, lens, refs[:n], a, g, up, down)

    sides = []
    for i, (width, side) in enumerate(((uwp, urp), (dwp, drp))):
        big, rest = two_parts(width[...])
        wide2[i, :64, :] = big
        wide2[i, 64:, :] = rest
        sides.append(side[...])

    def examples(j, carry):
        for i, grad in enumerate((up, down)):
            pre = jnp.concatenate(
                [
                    precondition(grad[2 * j + k], moments[2 * i], moments[2 * i + 1])
                    for k in range(2)
                ],
                axis=0,
            )
            big, rest = two_parts(pre)
            both = lax.dot_general(big, wide2[i], nt, preferred_element_type=F32)
            small = lax.dot_general(rest, wide2[i], nt, preferred_element_type=F32)
            wide = both[:, :64] + (both[:, 64:] + (small[:, :64] + small[:, 64:]))
            for k in range(2):
                out[2 * j + k, i * 64 : (i + 1) * 64, :] = jnp.dot(
                    sides[i],
                    wide[k * 128 : (k + 1) * 128],
                    precision=lax.Precision.HIGHEST,
                    preferred_element_type=F32,
                )
        return carry

    lax.fori_loop(0, 3, examples, 0)


def final_grads(which, nblk, lens, pieces, a, g, moments, *projectors):
    return pl.pallas_call(
        functools.partial(final_kernel, which, nblk),
        out_shape=jax.ShapeDtypeStruct((6, 128, 64), F32),
        in_specs=[pl.BlockSpec(memory_space=SMEM)]
        + [pl.BlockSpec(memory_space=VMEM)] * (len(which) + 14),
        out_specs=pl.BlockSpec(memory_space=VMEM),
        scratch_shapes=[
            VMEM((6, 128, 512), F32),
            VMEM((6, 128, 512), F32),
            VMEM((4, 128, 512), F32),
            VMEM((2, 128, 512), BF16),
        ],
        compiler_params=pltpu.CompilerParams(vmem_limit_bytes=6 * MIB),
        cost_estimate=pl.CostEstimate(
            flops=4 * nblk * len(which) * BLK * 512 * 128,
            bytes_accessed=nblk * len(which) * BLK * 512,
            transcendentals=0,
        ),
    )(lens, *pieces, a, g, *moments, *projectors)


def shifts(first, s):
    pairs = []
    for core in range(2):
        for z in range(4):
            for y in range(4):
                along_y = (core == 0) == first
                to = (z, (y + s) % 4) if along_y else ((z + s) % 4, y)
                pairs.append((core * 16 + z * 4 + y, core * 16 + to[0] * 4 + to[1]))
    return pairs


def send(x, first, s):
    return x if s == 0 else lax.ppermute(x, ("core", "z", "y"), shifts(first, s))


def features(nb, lens, w, moments, a, g, projectors):
    rows, sub, step, per = nb * BLK // 4, nb * BLK // 16, 32, nb // 4
    got = [None] * 4
    coded = far_piece(lens, w, a, g, per, 2)
    got[2] = send(coded, True, 2)
    coded, a, g = lax.optimization_barrier((coded, a, g))
    a, g = load(a, g)
    for s in (1, 3):
        got[s] = send(partial_piece(lens, w, a, g, per, s), True, s)
    got[2], own_lens = lax.optimization_barrier((got[2], lens))
    got[0] = partial_piece(own_lens, w, a, g, per, 0)
    got[0], moments = lax.optimization_barrier((got[0], moments))
    ring = ring_of(moments)
    back = [None] * 4
    for which in ((2,), (1, 3, 0)):
        for s, mid in zip(which, middle_sum(got, rows, sub, step, which)):
            back[s] = send(mid, False, s)
    own = last_sum(back, sub, step)
    piece = join([send(own, False, s) for s in range(4)])
    pieces = {s: send(piece, True, s) for s in (0, 1, 3, 2)}
    which = (0, 1, 3, 2)
    return final_grads(which, per, lens, [pieces[s] for s in which], a, g, ring, *projectors)


def share(x, axes, n):
    return lax.all_to_all(jnp.broadcast_to(x[None], (n,) + x.shape), axes, 0, 0, tiled=True)


def length_rows(lengths, rank, width):
    rows = jnp.stack([lengths // 64, lengths % 64])
    return jnp.pad(rows, ((0, rank - 2), (0, width - lengths.shape[0]))).astype(BF16)


def blocks_needed(rows, n):
    pairs = jnp.stack([r[2, :2, :n] for r in rows]).astype(F32)
    lengths = (pairs[:, 0] * 64.0 + pairs[:, 1]).astype(I32)
    return jnp.max(jnp.sum((lengths + (BLK - 1)) // BLK, axis=1))


def body(a, g, lengths, sf, ef, sra, srv, era, erv, urp, uwp, dwp, drp):
    param = ("z", "y")
    mine = jnp.stack([sf.T, ef, length_rows(lengths, sf.shape[1], sf.shape[0])])
    rows = ring_of(mine)
    w = turn(rows)
    moments = jnp.concatenate([era, erv, sra.T, srv.T], axis=0)
    projectors = (urp.T, uwp.T, dwp.T, drp.T)
    most = a.shape[0] * a.shape[1] // BLK
    sizes = [80, most]
    need = blocks_needed(rows, lengths.shape[0])
    which = sum((need > nb).astype(I32) for nb in sizes[:-1])
    part = lax.switch(
        which,
        [functools.partial(features, nb) for nb in sizes],
        lengths,
        w,
        moments,
        a,
        g,
        projectors,
    )
    owned = jnp.swapaxes(part.reshape(6, 16, 8, 64), 0, 1)
    raw = jnp.sum(lax.all_to_all(owned, param, 0, 0, tiled=True), axis=0)
    square = jnp.sum(raw * raw, axis=(1, 2))
    square = share(jnp.broadcast_to(square[:, None], (6, 128)), param, 16)
    scale = lax.rsqrt(jnp.sum(square, axis=0)[:, 0] / 8192.0 + 1e-06)
    return (raw * scale[:, None, None]).reshape(6, 512)


def solution(mesh):
    grid = Mesh(mesh.devices.reshape(4, 2, 4, 4), ("x", "core", "z", "y"))
    dp, param = ("x", "core"), ("z", "y")
    in_specs = (
        P(dp, None, param),
        P(dp, None, param),
        P(dp),
        P(param, dp),
        P(dp, param),
        P(param, dp),
        P(param, dp),
        P(dp, param),
        P(dp, param),
        P(),
        P(param, None),
        P(param, None),
        P(),
    )
    return jax.shard_map(body, mesh=grid, in_specs=in_specs, out_specs=P(dp, param), check_vma=False)
```
